256 devices in a mesh: grp: 2 (over core), gx: 16 (over x_lo, z), gy: 8 (over y, x_hi).
Axes of the slice: x: 4 (x_hi: 2, x_lo: 2; x = x_hi * 2 + x_lo), y: 4, z: 8, core: 2. Of those that a mesh axis runs over, the one named last changes fastest.
Arguments:
- velocity: float32 [3, 128, 128, 128], P(None, 'gx', ('grp', 'gy')), may hold values from -6 to 6
- moments: float32 [64, 128, 128, 128], P(None, 'gx', ('grp', 'gy')), may hold values from 0.1 to 1
- field: float32 [3, 128, 128, 128], P(None, 'gx', ('grp', 'gy')), may hold values from -6 to 6
- material: int32 [128, 128, 128], P('gx', ('grp', 'gy')), may hold values 0 or 1
- nozzle: int32 [256], replicated, may hold values from 0 to 2097025, as said below
- jet: float32 [3], replicated, may hold values from -2 to 2
- inlet: float32 [64], replicated, may hold values from 0.2 to 1
- rates: float32 [64, 32], replicated, may hold values from 0.02 to 0.8
- partners: int32 [64, 32], replicated, may hold values from 0 to 63
Outputs:
- new_velocity: float32 [3, 128, 128, 128], P(None, 'gx', ('grp', 'gy'))
- new_moments: float32 [64, 128, 128, 128], P(None, 'gx', ('grp', 'gy'))
The draws below stay inside these ranges and needn't reach their ends.
Inputs may be any that keep to these rules, and one draw needn't show every extreme that they name: `nozzle`: distinct cells of the two layers at z = 0 and 1: each entry is (x * 128 + y) * 128 + z with z 0 or 1.
All inputs are finite; a program needn't handle non-finite values. No bound on the sum of `material` on one device may be relied on, other than what follows from the above.
Results may differ from the reference program's by a relative error of at most 0.0032.
Values sent between devices are 32-bit elements; how exact they have to be, the bound alone decides.
A program may use at most 128 MiB of HBM per device.

```python
import math
import jax
import jax.numpy as jnp
from jax import lax

M = 64
R = 32
NZ = 128
NOZ = 256
NX = 128
NY = 128


def draw_nozzle(key, part):
    shuffled = jax.random.permutation(key, 2 * NX * NY - 2) + 1
    extremes = jnp.array([0, 2 * NX * NY - 1], dtype=jnp.int32)
    chosen = jnp.concatenate([extremes, shuffled[:NOZ - 2].astype(jnp.int32)])
    return (chosen // 2 * NZ + chosen % 2).astype(jnp.int32)


def rough_values(key):
    return 0.8 * jax.random.truncated_normal(key, -2.5, 2.5, (3, NX, NY, NZ), jnp.float32)


def steady_bounds():
    return 1.0


def smooth_modes(key):
    lengths_drawn = jax.random.uniform(jax.random.fold_in(key, 1), (3, 3, 3), jnp.float32)
    signs_drawn = jax.random.uniform(jax.random.fold_in(key, 2), (3, 3, 3), jnp.float32)
    phases = jax.random.uniform(jax.random.fold_in(key, 3), (3, 3), jnp.float32, 0.0, 2.0 * math.pi)
    wavelengths = 16.0 * jnp.exp(lengths_drawn * math.log(4.0))
    waves = jnp.where(signs_drawn < 0.5, -1.0, 1.0) * (2.0 * math.pi) / wavelengths
    coord_x = jnp.arange(NX, dtype=jnp.float32)
    coord_y = jnp.arange(NY, dtype=jnp.float32)
    coord_z = jnp.arange(NZ, dtype=jnp.float32)
    total = jnp.zeros((3, NX, NY, NZ), jnp.float32)
    for number in range(3):
        angle = waves[:, number, 0][:, None, None, None] * coord_x[None, :, None, None] + waves[:, number, 1][:, None, None, None] * coord_y[None, None, :, None] + waves[:, number, 2][:, None, None, None] * coord_z[None, None, None, :] + phases[:, number][:, None, None, None]
        total = total + 0.5 * jnp.sin(angle)
    return total


def draw_velocity(key, part):
    rough_part = rough_values(jax.random.fold_in(key, 11))
    numbers_drawn = jax.random.uniform(jax.random.fold_in(key, 12), (4,), jnp.float32)
    smooth_part = smooth_modes(jax.random.fold_in(key, 13))
    lowest = steady_bounds()
    direction_sign = jnp.where(numbers_drawn[3] < 0.5, -1.0, 1.0)
    steady_part = jnp.stack([numbers_drawn[0] - 0.5, numbers_drawn[1] - 0.5, direction_sign * (lowest + numbers_drawn[2])])
    return rough_part + smooth_part + steady_part[:, None, None, None]


def draw_field(key, part):
    rough_part = rough_values(jax.random.fold_in(key, 21))
    numbers_drawn = jax.random.uniform(jax.random.fold_in(key, 22), (3,), jnp.float32)
    smooth_part = smooth_modes(jax.random.fold_in(key, 23))
    lowest = steady_bounds()
    turning = numbers_drawn[0] * (2.0 * math.pi)
    strength = lowest + numbers_drawn[1]
    steady_part = jnp.stack([strength * jnp.cos(turning), strength * jnp.sin(turning), numbers_drawn[2] - 0.5])
    return rough_part + smooth_part + steady_part[:, None, None, None]


def with_ends(entries, key, smallest, largest):
    shape = entries.shape
    spot = [jax.random.randint(jax.random.fold_in(key, axis), (), 0, shape[axis]) for axis in range(len(shape))]
    entries = entries.at[tuple(spot)].set(smallest)
    longest = shape.index(max(shape))
    spot[longest] = (spot[longest] + 1) % shape[longest]
    return entries.at[tuple(spot)].set(largest)


def levels(key, shape, shards, smallest, high):
    def one(dim, parts):
        steps = jax.random.uniform(jax.random.fold_in(jax.random.fold_in(key, 6), dim), (parts,), jnp.float32, smallest / len(shards), high / len(shards))
        return jnp.repeat(jnp.exp(steps), shape[dim] // parts).reshape((-1,) + (1,) * (len(shape) - dim - 1))

    loudness = one(*shards[0])
    for cut in shards[1:]:
        loudness = loudness * one(*cut)
    return loudness


def setup_inputs(seed: int = 0) -> dict:
    arg_keys = jax.random.split(jax.random.key(seed), 10)
    velocity = draw_velocity(jax.random.fold_in(arg_keys[9], 71), 0)
    moments = jnp.clip(jnp.exp(math.log(1.0) - 2.3025851 * jax.random.uniform(arg_keys[1], (M, NX, NY, NZ), jnp.float32) ** levels(arg_keys[1], (M, NX, NY, NZ), ((1, 16), (2, 16)), -0.2, 0.2)), 0.1, 1.0)
    field = draw_field(jax.random.fold_in(arg_keys[9], 71), 0)
    material = with_ends((jax.random.randint(arg_keys[3], (NX, NY, NZ), 0, 8) < 7).astype(jnp.int32), jax.random.fold_in(arg_keys[3], 1), 0, 1)
    nozzle = draw_nozzle(jax.random.fold_in(arg_keys[9], 71), 0)
    jet = jnp.clip(jax.random.uniform(arg_keys[5], (3,), jnp.float32, -2.0, 2.0), -2.0, 2.0)
    inlet = jnp.clip(jnp.exp(jax.random.uniform(arg_keys[6], (M,), jnp.float32, math.log(0.2), math.log(1.0))), 0.2, 1.0)
    rates = jnp.clip(jnp.exp(jax.random.uniform(arg_keys[7], (M, R), jnp.float32, math.log(0.02), math.log(0.8))), 0.02, 0.8)
    partners = with_ends(jax.random.randint(arg_keys[8], (M, R), 0, M), jax.random.fold_in(arg_keys[8], 1), 0, M - 1).astype(jnp.int32)
    return dict(velocity=velocity, moments=moments, field=field, material=material, nozzle=nozzle, jet=jet, inlet=inlet, rates=rates, partners=partners)


step_size = 0.2
viscosity = 0.5
screening = 0.0001


def neighbour(values, direction, offset):
    widths = [(0, 0)] * values.ndim
    widths[direction] = (1, 1)
    padded = jnp.pad(values, widths)
    return lax.slice_in_dim(padded, 1 + offset, 1 + offset + values.shape[direction], axis=direction)


def central(values, direction):
    return (neighbour(values, direction, 1) - neighbour(values, direction, -1)) * 0.5


def cross_product(first_field, second_field):
    return jnp.stack([first_field[1] * second_field[2] - first_field[2] * second_field[1],
                      first_field[2] * second_field[0] - first_field[0] * second_field[2],
                      first_field[0] * second_field[1] - first_field[1] * second_field[0]])


def upwind(density, speed_part, direction):
    widths = [(0, 0)] * density.ndim
    widths[direction] = (1, 1)
    density_pad = jnp.pad(density, widths)
    speed_pad = jnp.pad(speed_part, widths)
    length = density.shape[direction]
    face_speed = 0.5 * (lax.slice_in_dim(speed_pad, 0, length + 1, axis=direction)
                        + lax.slice_in_dim(speed_pad, 1, length + 2, axis=direction))
    face_flux = (jnp.maximum(face_speed, 0.0) * lax.slice_in_dim(density_pad, 0, length + 1, axis=direction)
                 + jnp.minimum(face_speed, 0.0) * lax.slice_in_dim(density_pad, 1, length + 2, axis=direction))
    return lax.slice_in_dim(face_flux, 1, length + 1, axis=direction) - lax.slice_in_dim(face_flux, 0, length, axis=direction)


def wave_factor(length, sample):
    waves = jnp.arange(length)
    return 2.0 - 2.0 * jnp.cos(waves.astype(sample.dtype) * (2.0 * jnp.pi / length))


def potential_of(source):
    size_x, size_y, size_z = source.shape
    padded = jnp.zeros((2 * size_x, 2 * size_y, 2 * size_z), source.dtype)
    padded = padded.at[:size_x, :size_y, :size_z].set(source)
    spectrum = jnp.fft.fftn(padded)
    factor = (screening + wave_factor(2 * size_x, source)[:, None, None]
              + wave_factor(2 * size_y, source)[None, :, None]
              + wave_factor(2 * size_z, source)[None, None, :])
    result = jnp.fft.ifftn(spectrum * (-1.0 / factor)).real
    return result[:size_x, :size_y, :size_z].astype(source.dtype)


def growth_terms(moments, rates, partners):
    classes = moments.shape[0]
    partner_count = partners.shape[1]
    narrow = lax.optimization_barrier(moments.astype(jnp.bfloat16))
    owner = (jnp.arange(classes * partner_count) // partner_count).astype(jnp.int32)
    partner_flat = partners.reshape(-1).astype(jnp.int32)
    target = jnp.minimum(classes - 1, jnp.maximum(owner, partner_flat) + 1)
    rate_flat = rates.reshape(-1)

    def slab_terms(position):
        columns = lax.dynamic_index_in_dim(narrow, position, 1, keepdims=False)
        columns = columns.reshape(classes, -1).astype(rates.dtype)
        pair_rate = (rate_flat[:, None] * columns[owner]) * columns[partner_flat]
        pair_rate = lax.optimization_barrier(pair_rate.astype(jnp.bfloat16)).astype(rates.dtype)
        gained = jax.ops.segment_sum(pair_rate, target, num_segments=classes)
        removed = jnp.sum(pair_rate.reshape(classes, partner_count, -1), axis=1)
        return (gained - removed).reshape(classes, moments.shape[2], moments.shape[3])

    per_slab = lax.map(slab_terms, jnp.arange(moments.shape[1]))
    return jnp.moveaxis(per_slab, 0, 1)


def reference(velocity, moments, field, material, nozzle, jet, inlet, rates, partners):
    liquid = material.astype(velocity.dtype)
    moving = velocity * liquid
    current = cross_product(moving, field)
    source = central(current[0], 0) + central(current[1], 1) + central(current[2], 2)
    potential = potential_of(source)
    gradient = jnp.stack([central(potential, 0), central(potential, 1), central(potential, 2)])
    lorentz = cross_product(current - gradient, field)
    spread = ((neighbour(moving, 1, 1) + neighbour(moving, 1, -1))
              + (neighbour(moving, 2, 1) + neighbour(moving, 2, -1))
              + (neighbour(moving, 3, 1) + neighbour(moving, 3, -1)) - 6.0 * moving)
    new_velocity = liquid * (moving + step_size * (lorentz + viscosity * spread))
    nozzle_x = nozzle // (NY * NZ)
    nozzle_y = (nozzle // NZ) % NY
    nozzle_z = nozzle % NZ
    count_cells = nozzle.shape[0]
    new_velocity = new_velocity.at[:, nozzle_x, nozzle_y, nozzle_z].set(
        jnp.broadcast_to(jet[:, None], (3, count_cells)))
    growth = growth_terms(moments, rates, partners)

    def transport_class(density):
        return upwind(density, moving[0], 0) + upwind(density, moving[1], 1) + upwind(density, moving[2], 2)

    transport = lax.map(transport_class, moments)
    new_moments = moments + step_size * liquid * (growth - transport)
    new_moments = new_moments.at[:, nozzle_x, nozzle_y, nozzle_z].set(
        jnp.broadcast_to(inlet[:, None], (inlet.shape[0], count_cells)))
    return (new_velocity, new_moments)
```

```python
import functools
import math

import jax
import jax.numpy as jnp
import numpy as np
from jax import lax
from jax.experimental import pallas as pl
from jax.experimental.pallas import tpu as pltpu
from jax.sharding import PartitionSpec as P

step_size = 0.2
viscosity = 0.5
screening = 0.0001
MESH = pl.DeviceIdType.MESH
SIDE = 8
PITCH = 10
SLOTS = 16
LANES = 128


def wave_of(length):
    index = np.arange(2 * length)
    return np.where(index <= length, index, index - length)


def real_basis(length):
    span = 2 * length
    index = np.arange(span)
    angle = 2.0 * math.pi / span * ((wave_of(length)[:, None] * np.arange(length)[None, :]) % span)
    return np.where(index[:, None] <= length, np.cos(angle), np.sin(angle))


def real_weights(length):
    span = 2 * length
    weights = np.full(span, 2.0 / span)
    weights[0] = weights[length] = 1.0 / span
    return weights


def wave_factors(length):
    return 2.0 - 2.0 * np.cos(2.0 * math.pi * wave_of(length) / (2 * length))


def tables(full_x, full_y, depth):
    bricks_x, bricks_y = full_x // SIDE, full_y // SIDE
    basis_x, basis_y, basis_z = real_basis(full_x), real_basis(full_y), real_basis(depth)
    inverse_x = basis_x * real_weights(full_x)[:, None]
    inverse_y = basis_y * real_weights(full_y)[:, None]
    inverse_z = basis_z * real_weights(depth)[:, None]
    forward_x = np.zeros((2 * full_x, bricks_x * SLOTS))
    backward_x = np.zeros((bricks_x * SLOTS, 2 * full_x))
    for brick in range(bricks_x):
        for slot in range(PITCH):
            x = SIDE * brick + (slot if slot < SIDE else (-1 if slot == SIDE else SIDE))
            if 0 <= x < full_x:
                forward_x[:, brick * SLOTS + slot] = basis_x[:, x]
                backward_x[brick * SLOTS + slot] = inverse_x[:, x]
    masks = np.zeros((bricks_y, SLOTS, LANES))
    for brick in range(bricks_y):
        for slot in range(PITCH):
            for lane in range(LANES):
                source = (lane - (SIDE * brick - 1)) % LANES
                if slot < SIDE:
                    y = SIDE * brick - 1 + source - PITCH * slot
                    inside = 0 <= source - PITCH * slot < PITCH
                else:
                    offset = source - PITCH * SIDE - SIDE * (slot - SIDE)
                    y = SIDE * brick + offset
                    inside = 0 <= offset < SIDE
                if inside and 0 <= y < full_y:
                    masks[brick, slot, lane] = 1.0
    f32 = lambda array: jnp.asarray(np.asarray(array, np.float32))
    return dict(
        basis_z=f32(basis_z),
        inverse_z=f32(inverse_z),
        forward_x=f32(forward_x),
        backward_x=f32(backward_x),
        forward_y=f32(basis_y.T),
        backward_y=f32(inverse_y),
        factor_x=f32(wave_factors(full_x)[:, None]),
        factor_y=f32(wave_factors(full_y)[None, :]),
        factor_z=f32(wave_factors(depth) + screening),
        masks=f32(masks.reshape(bricks_y * SLOTS, LANES)),
    )


def turn_of(slot):
    return (-PITCH * slot if slot < SIDE else 1 - PITCH * SIDE - SIDE * (slot - SIDE)) % LANES


def roll(values, shift, axis):
    shift = shift % values.shape[axis]
    return values if shift == 0 else pltpu.roll(values, shift, axis)


def dot(first, second, dims=((1,), (0,))):
    return lax.dot_general(
        first,
        second,
        (dims, ((), ())),
        precision=lax.Precision.HIGHEST,
        preferred_element_type=jnp.float32,
    )


def kernel(
    velocity, field, material, moments, nozzle, jet, inlet, rates, partners,
    basis_z, inverse_z, forward_x, backward_x, forward_y, backward_y,
    factor_x, factor_y, factor_z, masks,
    new_velocity, new_moments,
    ext, grown, result, face_x, face_y, cut_y, coef,
    source, send_a, recv_a, send_b, recv_b, send_c, recv_c, send_d, recv_d, poten,
    load_sem, store_sem, halo_send, halo_recv, ssem, rsem,
):
    wide = 16
    classes = rates.shape[0]
    rows = SIDE * SIDE
    me_x = lax.axis_index("gx")
    me_grp, me_gy = lax.axis_index("grp"), lax.axis_index("gy")
    groups = lax.axis_size("gy")
    me_y = me_grp * groups + me_gy

    def along_x(index):
        return {"gx": index}

    def along_y(index):
        return {"grp": index // groups, "gy": lax.rem(index, groups)}

    load = pltpu.make_async_copy(moments, ext.at[pl.ds(0, classes)], load_sem)
    load.start()
    barrier = pltpu.get_barrier_semaphore()

    @pl.loop(1, wide)
    def _(step):
        pl.semaphore_signal(
            barrier, inc=1, device_id=along_x(lax.rem(me_x + step, wide)), device_id_type=MESH
        )
        pl.semaphore_signal(
            barrier, inc=1, device_id=along_y(lax.rem(me_y + step, wide)), device_id_type=MESH
        )

    lane = lax.broadcasted_iota(jnp.int32, (SIDE, LANES), 1)
    row = lax.broadcasted_iota(jnp.int32, (SIDE, LANES), 0)
    not_first, not_last = lane != 0, lane != LANES - 1

    def up_z(v):
        return jnp.where(not_last, roll(v, -1, 1), 0.0)

    def down_z(v):
        return jnp.where(not_first, roll(v, 1, 1), 0.0)

    def current_at(x):
        m = [ext[classes + a, SIDE * x : SIDE * x + SIDE] for a in range(3)]
        f = [field[a, x] for a in range(3)]
        return (
            m[1] * f[2] - m[2] * f[1],
            m[2] * f[0] - m[0] * f[2],
            m[0] * f[1] - m[1] * f[0],
        )

    for x in range(SIDE):
        liquid = material[x].astype(jnp.float32)
        for a in range(3):
            ext[classes + a, SIDE * x : SIDE * x + SIDE] = velocity[a, x] * liquid
    currents = [current_at(x) for x in range(SIDE)]
    for x in range(SIDE):
        c1, c2 = currents[x][1], currents[x][2]
        s = jnp.where(row < SIDE - 1, roll(c1, -1, 0), 0.0) - jnp.where(row > 0, roll(c1, 1, 0), 0.0)
        s = s + up_z(c2) - down_z(c2)
        if x + 1 < SIDE:
            s = s + currents[x + 1][0]
        if x > 0:
            s = s - currents[x - 1][0]
        source[PITCH * x + 1 : PITCH * x + 1 + SIDE] = 0.5 * s
        source[PITCH * x : PITCH * x + 1] = 0.5 * c1[0:1]
        source[PITCH * x + PITCH - 1 : PITCH * x + PITCH] = -0.5 * c1[SIDE - 1 : SIDE]
    edge = PITCH * SIDE
    source[edge : edge + SIDE] = 0.5 * currents[0][0]
    source[edge + SIDE : edge + 2 * SIDE] = -0.5 * currents[SIDE - 1][0]
    source[edge + 2 * SIDE :] = jnp.zeros((LANES - edge - 2 * SIDE, LANES), jnp.float32)
    send_a[...] = dot(basis_z[...], source[...], ((1,), (1,)))

    pl.semaphore_wait(barrier, 2 * (wide - 1))

    def exchange(phase, send, recv, me, target):
        mine = pl.ds(pl.multiple_of(me * wide, wide), wide)

        def start(step):
            other = lax.rem(me + step, wide)
            pltpu.make_async_remote_copy(
                src_ref=send.at[pl.ds(pl.multiple_of(other * wide, wide), wide)],
                dst_ref=recv.at[mine],
                send_sem=ssem.at[phase],
                recv_sem=rsem.at[phase],
                device_id=target(other),
                device_id_type=MESH,
            ).start()

        pl.loop(1, wide)(start)
        recv[mine] = send[mine]

    def arrived(phase, send, recv):
        part = pl.ds(0, (wide - 1) * wide)
        pltpu.make_async_copy(recv.at[part], recv.at[part], rsem.at[phase]).wait()

    def sent(phase, send):
        part = pl.ds(0, (wide - 1) * wide)
        pltpu.make_async_copy(send.at[part], send.at[part], ssem.at[phase]).wait()

    exchange(0, send_a, recv_a, me_y, along_y)

    load.wait()
    flat = ext.reshape((classes + 3) * rows, LANES)
    for side in range(2):
        cut_y[side] = flat[pl.ds(side * (SIDE - 1), (classes + 3) * SIDE, stride=SIDE), :].reshape(
            classes + 3, SIDE, LANES
        )
    lower_x, upper_x = lax.rem(me_x + wide - 1, wide), lax.rem(me_x + 1, wide)
    lower_y, upper_y = lax.rem(me_y + wide - 1, wide), lax.rem(me_y + 1, wide)
    halos = []
    for number, (src, dst, device) in enumerate(
        [
            (cut_y.at[0], face_y.at[1], along_y(lower_y)),
            (cut_y.at[1], face_y.at[0], along_y(upper_y)),
            (ext.at[:, pl.ds(0, SIDE)], face_x.at[1], along_x(lower_x)),
            (ext.at[:, pl.ds(rows - SIDE, SIDE)], face_x.at[0], along_x(upper_x)),
        ]
    ):
        copy = pltpu.make_async_remote_copy(
            src_ref=src,
            dst_ref=dst,
            send_sem=halo_send.at[number],
            recv_sem=halo_recv.at[number],
            device_id=device,
            device_id_type=MESH,
        )
        copy.start()
        halos.append(copy)

    square = lax.broadcasted_iota(jnp.int32, (classes, LANES), 1)
    owner = lax.broadcasted_iota(jnp.int32, (classes, LANES), 0)
    full = jnp.zeros((classes, LANES), jnp.float32)
    for r in range(rates.shape[1]):
        full = full + jnp.where(partners[:, r : r + 1] == square, rates[:, r : r + 1], 0.0)
    turned = jnp.concatenate([full, jnp.zeros((LANES - classes, LANES), jnp.float32)], 0).T[:classes]
    low = jnp.where(square < owner, full + turned, jnp.where(square == owner, full, 0.0))
    full = full - jnp.where(owner == classes - 1, low, 0.0)
    low = jnp.where(owner > 0, roll(low, 1, 0), 0.0)
    both = jnp.concatenate([low, full], 0)
    high_part = both.astype(jnp.bfloat16).astype(jnp.float32)
    low_part = both - high_part
    column = lax.broadcasted_iota(jnp.int32, (2 * classes, LANES), 1)
    weights = jnp.where(column < classes, high_part, roll(low_part, classes, 1)).astype(jnp.bfloat16)
    flat_grown = grown.reshape(classes * rows, LANES)

    def grow(pair):
        parts = [
            flat[pl.ds(2 * pair + h, classes, stride=rows), :].astype(jnp.bfloat16) for h in range(2)
        ]
        narrow = jnp.concatenate(parts, 1)
        mixed = jnp.dot(
            weights, jnp.concatenate([narrow, narrow], 0), preferred_element_type=jnp.float32
        )
        for h in range(2):
            n = parts[h].astype(jnp.float32)
            piece = mixed[:, h * LANES : (h + 1) * LANES]
            flat_grown[pl.ds(2 * pair + h, classes, stride=rows), :] = (
                roll(n, 1, 0) * piece[:classes] - n * piece[classes:]
            )

    pl.loop(0, rows // 2)(grow)

    cell = lax.broadcasted_iota(jnp.int32, (rows, 1), 0)
    full_y = SIDE * wide
    base = ((me_x * SIDE + cell // SIDE) * full_y + me_y * SIDE + cell % SIDE) * LANES
    hit = [
        jnp.max(jnp.where(nozzle[...] == base + z, 1.0, 0.0), axis=1, keepdims=True) for z in range(2)
    ]
    deep = lax.broadcasted_iota(jnp.int32, (rows, LANES), 1)
    coef[8] = jnp.where(deep == 0, hit[0], jnp.where(deep == 1, hit[1], 0.0))

    arrived(0, send_a, recv_a)
    strips = [jnp.zeros((wide, LANES), jnp.float32) for _ in range(PITCH)]
    for by in range(wide):
        line = roll(recv_a[by * wide : (by + 1) * wide], SIDE * by - 1, 1)
        for slot in range(PITCH):
            strips[slot] = strips[slot] + line * masks[by * SLOTS + slot : by * SLOTS + slot + 1]
    for slot in range(SLOTS):
        send_b[pl.ds(slot, wide, stride=SLOTS), :] = (
            roll(strips[slot], turn_of(slot), 1)
            if slot < PITCH
            else jnp.zeros((wide, LANES), jnp.float32)
        )
    exchange(1, send_b, recv_b, me_x, along_x)

    wave = factor_z[me_y * wide + me_x]
    inverse = -1.0 / ((factor_x[...] + wave) + factor_y[...])
    arrived(1, send_b, recv_b)
    plane = dot(dot(forward_x[...], recv_b[...]), forward_y[...]) * inverse
    send_c[...] = dot(backward_x[...], dot(plane, backward_y[...]))
    exchange(2, send_c, recv_c, me_x, along_x)
    arrived(2, send_c, recv_c)
    strips = [
        roll(recv_c[pl.ds(slot, wide, stride=SLOTS), :], -turn_of(slot), 1) for slot in range(PITCH)
    ]
    for by in range(wide):
        total = jnp.zeros((wide, LANES), jnp.float32)
        for slot in range(PITCH):
            total = total + strips[slot] * masks[by * SLOTS + slot : by * SLOTS + slot + 1]
        send_d[by * wide : (by + 1) * wide] = roll(total, 1 - SIDE * by, 1)
    exchange(3, send_d, recv_d, me_y, along_y)

    for copy in halos:
        copy.wait_recv()
    has_x = [(me_x > 0).astype(jnp.float32), (me_x < wide - 1).astype(jnp.float32)]
    has_y = [(me_y > 0).astype(jnp.float32), (me_y < wide - 1).astype(jnp.float32)]

    def moving_at(a, x):
        if x < 0:
            return face_x[0, classes + a] * has_x[0]
        if x >= SIDE:
            return face_x[1, classes + a] * has_x[1]
        return ext[classes + a, SIDE * x : SIDE * x + SIDE]

    def around_y(a, x):
        here = moving_at(a, x)
        below = jnp.where(row == 0, face_y[0, classes + a, x : x + 1] * has_y[0], roll(here, 1, 0))
        above = jnp.where(
            row == SIDE - 1, face_y[1, classes + a, x : x + 1] * has_y[1], roll(here, -1, 0)
        )
        return below, above

    for x in range(SIDE):
        part = slice(SIDE * x, SIDE * x + SIDE)
        stop = coef[8, part]
        scale = step_size * material[x].astype(jnp.float32) * (1.0 - stop)
        total = jnp.zeros((SIDE, LANES), jnp.float32)
        for a in range(3):
            here = moving_at(a, x)
            if a == 0:
                below, above = moving_at(0, x - 1), moving_at(0, x + 1)
            elif a == 1:
                below, above = around_y(1, x)
            else:
                below, above = down_z(here), up_z(here)
            up, down = 0.5 * (here + above), 0.5 * (below + here)
            total = total + (jnp.maximum(up, 0.0) - jnp.minimum(down, 0.0))
            plus, minus = -scale * jnp.minimum(up, 0.0), scale * jnp.maximum(down, 0.0)
            if a == 0:
                if x == 0:
                    minus = minus * has_x[0]
                if x == SIDE - 1:
                    plus = plus * has_x[1]
            elif a == 1:
                minus = jnp.where(row == 0, minus * has_y[0], minus)
                plus = jnp.where(row == SIDE - 1, plus * has_y[1], plus)
            else:
                minus = jnp.where(not_first, minus, 0.0)
                plus = jnp.where(not_last, plus, 0.0)
            coef[2 * a + 1, part] = minus
            coef[2 * a + 2, part] = plus
        coef[0, part] = 1.0 - stop - scale * total
        coef[7, part] = scale

    def advance(k):
        fill = inlet[k]
        for x in range(SIDE):
            part = slice(SIDE * x, SIDE * x + SIDE)
            here = ext[k, part]
            below = face_x[0, k] if x == 0 else ext[k, SIDE * x - SIDE : SIDE * x]
            above = face_x[1, k] if x == SIDE - 1 else ext[k, SIDE * x + SIDE : SIDE * x + 2 * SIDE]
            left = jnp.where(row == 0, face_y[0, k, x : x + 1], roll(here, 1, 0))
            right = jnp.where(row == SIDE - 1, face_y[1, k, x : x + 1], roll(here, -1, 0))
            result[k, part] = (
                (coef[0, part] * here + coef[7, part] * grown[k, part])
                + (coef[1, part] * below + coef[2, part] * above)
                + (coef[3, part] * left + coef[4, part] * right)
                + (coef[5, part] * roll(here, 1, 1) + coef[6, part] * roll(here, -1, 1))
                + coef[8, part] * fill
            )

    pl.loop(0, classes)(advance)
    store = pltpu.make_async_copy(result, new_moments, store_sem)
    store.start()

    arrived(3, send_d, recv_d)
    poten[...] = dot(recv_d[...], inverse_z[...], ((0,), (0,)))
    for x in range(SIDE):
        part = slice(SIDE * x, SIDE * x + SIDE)

        def pot(x):
            if x < 0:
                return poten[edge : edge + SIDE]
            if x >= SIDE:
                return poten[edge + SIDE : edge + 2 * SIDE]
            return poten[PITCH * x + 1 : PITCH * x + 1 + SIDE]

        low_y = poten[PITCH * x : PITCH * x + SIDE]
        high_y = poten[PITCH * x + 2 : PITCH * x + 2 + SIDE]
        middle = pot(x)
        gradient = (
            0.5 * (pot(x + 1) - pot(x - 1)),
            0.5 * (high_y - low_y),
            0.5 * (up_z(middle) - down_z(middle)),
        )
        c = current_at(x)
        d = [c[a] - gradient[a] for a in range(3)]
        f = [field[a, x] for a in range(3)]
        lorentz = (d[1] * f[2] - d[2] * f[1], d[2] * f[0] - d[0] * f[2], d[0] * f[1] - d[1] * f[0])
        liquid = material[x].astype(jnp.float32)
        stop = coef[8, part] > 0.5
        for a in range(3):
            here = moving_at(a, x)
            below, above = around_y(a, x)
            spread = (
                (moving_at(a, x - 1) + moving_at(a, x + 1))
                + (below + above)
                + (down_z(here) + up_z(here))
                - 6.0 * here
            )
            value = liquid * (here + step_size * (lorentz[a] + viscosity * spread))
            new_velocity[a, x] = jnp.where(stop, jet[a], value)

    for phase, buffer in enumerate((send_a, send_b, send_c, send_d)):
        sent(phase, buffer)
    for copy in halos:
        copy.wait_send()
    store.wait()


def local(velocity, moments, field, material, nozzle, jet, inlet, rates, partners):
    width_x = lax.axis_size("gx")
    width_y = lax.axis_size("grp") * lax.axis_size("gy")
    cells_x, cells_y, depth = material.shape
    classes = moments.shape[0]
    rows = cells_x * cells_y
    table = tables(cells_x * width_x, cells_y * width_y, depth)
    vmem = pl.BlockSpec(memory_space=pltpu.VMEM)
    smem = pl.BlockSpec(memory_space=pltpu.SMEM)
    anywhere = pl.BlockSpec(memory_space=pl.ANY)
    f32 = jnp.float32
    square = pltpu.VMEM((2 * LANES, LANES), f32)
    new_velocity, new_moments = pl.pallas_call(
        kernel,
        out_shape=(
            jax.ShapeDtypeStruct(velocity.shape, f32),
            jax.ShapeDtypeStruct((classes, rows, depth), f32),
        ),
        in_specs=[vmem, vmem, vmem, anywhere, vmem, smem, smem, vmem, vmem]
        + [vmem] * 8 + [smem, vmem],
        out_specs=(vmem, anywhere),
        scratch_shapes=[
            pltpu.VMEM((classes + 3, rows, LANES), f32),
            pltpu.VMEM((classes, rows, LANES), f32),
            pltpu.VMEM((classes, rows, LANES), f32),
            pltpu.VMEM((2, classes + 3, SIDE, LANES), f32),
            pltpu.VMEM((2, classes + 3, SIDE, LANES), f32),
            pltpu.VMEM((2, classes + 3, SIDE, LANES), f32),
            pltpu.VMEM((9, rows, LANES), f32),
            pltpu.VMEM((LANES, LANES), f32),
            square, square, square, square, square, square, square, square,
            pltpu.VMEM((LANES, LANES), f32),
            pltpu.SemaphoreType.DMA,
            pltpu.SemaphoreType.DMA,
            pltpu.SemaphoreType.DMA((4,)),
            pltpu.SemaphoreType.DMA((4,)),
            pltpu.SemaphoreType.DMA((4,)),
            pltpu.SemaphoreType.DMA((4,)),
        ],
        compiler_params=pltpu.CompilerParams(
            collective_id=0, has_side_effects=True, vmem_limit_bytes=48 * 1024 * 1024
        ),
    )(
        velocity, field, material, moments.reshape(classes, rows, depth),
        nozzle.reshape(1, -1), jet, inlet, rates, partners,
        table["basis_z"], table["inverse_z"], table["forward_x"], table["backward_x"],
        table["forward_y"], table["backward_y"], table["factor_x"], table["factor_y"],
        table["factor_z"], table["masks"],
    )
    return (new_velocity, new_moments.reshape(moments.shape))


def solution(mesh):
    bricks = P(None, "gx", ("grp", "gy"), None)
    return jax.shard_map(
        local,
        mesh=mesh,
        in_specs=(bricks, bricks, bricks, P("gx", ("grp", "gy"), None), P(), P(), P(), P(), P()),
        out_specs=(bricks, bricks),
        check_vma=False,
    )
```

```python
import functools
import math

import jax
import jax.numpy as jnp
import numpy as np
from jax import lax
from jax.experimental import pallas as pl
from jax.experimental.pallas import tpu as pltpu
from jax.sharding import PartitionSpec as P

step_size = 0.2
viscosity = 0.5
screening = 0.0001
MESH = pl.DeviceIdType.MESH
SIDE = 8
PITCH = 10
SLOTS = 16
LANES = 128


def wave_of(length):
    index = np.arange(2 * length)
    return np.where(index <= length, index, index - length)


def real_basis(length):
    span = 2 * length
    index = np.arange(span)
    angle = 2.0 * math.pi / span * ((wave_of(length)[:, None] * np.arange(length)[None, :]) % span)
    return np.where(index[:, None] <= length, np.cos(angle), np.sin(angle))


def real_weights(length):
    span = 2 * length
    weights = np.full(span, 2.0 / span)
    weights[0] = weights[length] = 1.0 / span
    return weights


def wave_factors(length):
    return 2.0 - 2.0 * np.cos(2.0 * math.pi * wave_of(length) / (2 * length))


def tables(full_x, full_y, depth):
    bricks_x, bricks_y = full_x // SIDE, full_y // SIDE
    basis_x, basis_y, basis_z = real_basis(full_x), real_basis(full_y), real_basis(depth)
    inverse_x = basis_x * real_weights(full_x)[:, None]
    inverse_y = basis_y * real_weights(full_y)[:, None]
    inverse_z = basis_z * real_weights(depth)[:, None]
    forward_x = np.zeros((2 * full_x, bricks_x * SLOTS))
    backward_x = np.zeros((bricks_x * SLOTS, 2 * full_x))
    for brick in range(bricks_x):
        for slot in range(PITCH):
            x = SIDE * brick + (slot if slot < SIDE else (-1 if slot == SIDE else SIDE))
            if 0 <= x < full_x:
                forward_x[:, brick * SLOTS + slot] = basis_x[:, x]
                backward_x[brick * SLOTS + slot] = inverse_x[:, x]
    masks = np.zeros((bricks_y, SLOTS, LANES))
    for brick in range(bricks_y):
        for slot in range(PITCH):
            for lane in range(LANES):
                source = (lane - (SIDE * brick - 1)) % LANES
                if slot < SIDE:
                    y = SIDE * brick - 1 + source - PITCH * slot
                    inside = 0 <= source - PITCH * slot < PITCH
                else:
                    offset = source - PITCH * SIDE - SIDE * (slot - SIDE)
                    y = SIDE * brick + offset
                    inside = 0 <= offset < SIDE
                if inside and 0 <= y < full_y:
                    masks[brick, slot, lane] = 1.0
    f32 = lambda array: jnp.asarray(np.asarray(array, np.float32))
    return dict(
        basis_z=f32(basis_z),
        inverse_z=f32(inverse_z),
        forward_x=f32(forward_x),
        backward_x=f32(backward_x),
        forward_y=f32(basis_y.T),
        backward_y=f32(inverse_y),
        factor_x=f32(wave_factors(full_x)[:, None]),
        factor_y=f32(wave_factors(full_y)[None, :]),
        factor_z=f32(wave_factors(depth) + screening),
        masks=f32(masks.reshape(bricks_y * SLOTS, LANES)),
    )


def turn_of(slot):
    return (-PITCH * slot if slot < SIDE else 1 - PITCH * SIDE - SIDE * (slot - SIDE)) % LANES


def roll(values, shift, axis):
    shift = shift % values.shape[axis]
    return values if shift == 0 else pltpu.roll(values, shift, axis)


def dot(first, second, dims=((1,), (0,))):
    return lax.dot_general(
        first,
        second,
        (dims, ((), ())),
        precision=lax.Precision.HIGHEST,
        preferred_element_type=jnp.float32,
    )


def kernel(
    velocity_in, field_in, material_in, moments, nozzle_in, jet_in, inlet_in, rates_in, partners_in,
    basis_z_in, inverse_z_in, forward_x_in, backward_x_in, forward_y_in, backward_y_in,
    factor_x_in, factor_y_in, factor_z_in, masks_in,
    new_velocity, result,
    velocity, field, material, nozzle, jet, inlet, rates, partners,
    basis_z, inverse_z, forward_x, backward_x, forward_y, backward_y,
    factor_x, factor_y, factor_z, masks,
    ext, grown, face_x, face_y, cut_y, coef,
    edge_y, source, send_a, recv_a, send_b, recv_b, send_c, recv_c, send_d, recv_d, poten,
    load_sem, first_sem, later_sem, halo_send, halo_recv, ssem, rsem,
):
    wide = 16
    classes = rates.shape[1]
    rows = SIDE * SIDE
    me_x = lax.axis_index("gx")
    me_grp, me_gy = lax.axis_index("grp"), lax.axis_index("gy")
    groups = lax.axis_size("gy")
    me_y = me_grp * groups + me_gy

    def along_x(index):
        return {"gx": index}

    def along_y(index):
        return {"grp": index // groups, "gy": lax.rem(index, groups)}

    first = [
        pltpu.make_async_copy(src, dst, first_sem.at[number])
        for number, (src, dst) in enumerate(
            [(velocity_in, velocity), (field_in, field), (material_in, material), (basis_z_in, basis_z)]
        )
    ]
    load = pltpu.make_async_copy(moments, ext.at[pl.ds(0, classes)], load_sem)
    later = [
        pltpu.make_async_copy(src, dst, later_sem.at[number])
        for number, (src, dst) in enumerate(
            [
                (nozzle_in, nozzle), (jet_in, jet), (inlet_in, inlet), (rates_in, rates),
                (partners_in, partners), (inverse_z_in, inverse_z), (forward_x_in, forward_x),
                (backward_x_in, backward_x), (forward_y_in, forward_y), (backward_y_in, backward_y),
                (factor_x_in, factor_x), (factor_y_in, factor_y), (factor_z_in, factor_z),
                (masks_in, masks),
            ]
        )
    ]
    for copy in first + [load] + later:
        copy.start()
    barrier = pltpu.get_barrier_semaphore()

    @pl.loop(1, wide)
    def _(step):
        pl.semaphore_signal(
            barrier, inc=1, device_id=along_x(lax.rem(me_x + step, wide)), device_id_type=MESH
        )
        pl.semaphore_signal(
            barrier, inc=1, device_id=along_y(lax.rem(me_y + step, wide)), device_id_type=MESH
        )

    lane = lax.broadcasted_iota(jnp.int32, (SIDE, LANES), 1)
    row = lax.broadcasted_iota(jnp.int32, (SIDE, LANES), 0)
    not_first, not_last = lane != 0, lane != LANES - 1

    def up_z(v):
        return jnp.where(not_last, roll(v, -1, 1), 0.0)

    def down_z(v):
        return jnp.where(not_first, roll(v, 1, 1), 0.0)

    def current_at(x):
        m = [ext[classes + a, SIDE * x : SIDE * x + SIDE] for a in range(3)]
        f = [field[a, x] for a in range(3)]
        return (
            m[1] * f[2] - m[2] * f[1],
            m[2] * f[0] - m[0] * f[2],
            m[0] * f[1] - m[1] * f[0],
        )

    for copy in first:
        copy.wait()

    for x in range(SIDE):
        liquid = material[x].astype(jnp.float32)
        for a in range(3):
            ext[classes + a, SIDE * x : SIDE * x + SIDE] = velocity[a, x] * liquid
    currents = [current_at(x) for x in range(SIDE)]
    for x in range(SIDE):
        c1, c2 = currents[x][1], currents[x][2]
        s = jnp.where(row < SIDE - 1, roll(c1, -1, 0), 0.0) - jnp.where(row > 0, roll(c1, 1, 0), 0.0)
        s = s + up_z(c2) - down_z(c2)
        if x + 1 < SIDE:
            s = s + currents[x + 1][0]
        if x > 0:
            s = s - currents[x - 1][0]
        source[PITCH * x + 1 : PITCH * x + 1 + SIDE] = 0.5 * s
        source[PITCH * x : PITCH * x + 1] = 0.5 * c1[0:1]
        source[PITCH * x + PITCH - 1 : PITCH * x + PITCH] = -0.5 * c1[SIDE - 1 : SIDE]
    edge = PITCH * SIDE
    source[edge : edge + SIDE] = 0.5 * currents[0][0]
    source[edge + SIDE : edge + 2 * SIDE] = -0.5 * currents[SIDE - 1][0]
    source[edge + 2 * SIDE :] = jnp.zeros((LANES - edge - 2 * SIDE, LANES), jnp.float32)
    send_a[...] = dot(basis_z[...], source[...], ((1,), (1,)))

    pl.semaphore_wait(barrier, 2 * (wide - 1))

    def exchange(phase, send, recv, me, target):
        mine = pl.ds(pl.multiple_of(me * wide, wide), wide)

        def start(step):
            other = lax.rem(me + step, wide)
            pltpu.make_async_remote_copy(
                src_ref=send.at[pl.ds(pl.multiple_of(other * wide, wide), wide)],
                dst_ref=recv.at[mine],
                send_sem=ssem.at[phase],
                recv_sem=rsem.at[phase],
                device_id=target(other),
                device_id_type=MESH,
            ).start()

        pl.loop(1, wide)(start)
        recv[mine] = send[mine]

    def arrived(phase, send, recv):
        part = pl.ds(0, (wide - 1) * wide)
        pltpu.make_async_copy(recv.at[part], recv.at[part], rsem.at[phase]).wait()

    def sent(phase, send):
        part = pl.ds(0, (wide - 1) * wide)
        pltpu.make_async_copy(send.at[part], send.at[part], ssem.at[phase]).wait()

    flat = ext.reshape((classes + 3) * rows, LANES)
    lower_x, upper_x = lax.rem(me_x + wide - 1, wide), lax.rem(me_x + 1, wide)
    lower_y, upper_y = lax.rem(me_y + wide - 1, wide), lax.rem(me_y + 1, wide)

    def send_faces(begin, count, number):
        part = pl.ds(begin, count)
        for side in range(2):
            cut_y[side, part] = flat[
                pl.ds(begin * rows + side * (SIDE - 1), count * SIDE, stride=SIDE), :
            ].reshape(count, SIDE, LANES)
        copies = []
        for src, dst, device in (
            (cut_y.at[0, part], face_y.at[1, part], along_y(lower_y)),
            (cut_y.at[1, part], face_y.at[0, part], along_y(upper_y)),
            (ext.at[part, pl.ds(0, SIDE)], face_x.at[1, part], along_x(lower_x)),
            (ext.at[part, pl.ds(rows - SIDE, SIDE)], face_x.at[0, part], along_x(upper_x)),
        ):
            copy = pltpu.make_async_remote_copy(
                src_ref=src,
                dst_ref=dst,
                send_sem=halo_send.at[number],
                recv_sem=halo_recv.at[number],
                device_id=device,
                device_id_type=MESH,
            )
            copy.start()
            copies.append(copy)
            number += 1
        return copies

    exchange(0, send_a, recv_a, me_y, along_y)
    moving_faces = send_faces(classes, 3, 0)
    load.wait()
    moment_faces = send_faces(0, classes, 4)
    for copy in later:
        copy.wait()

    square = lax.broadcasted_iota(jnp.int32, (classes, LANES), 1)
    owner = lax.broadcasted_iota(jnp.int32, (classes, LANES), 0)
    label = lax.broadcasted_iota(jnp.int32, (classes, classes), 0)
    turned = jnp.zeros((classes, classes), jnp.float32)
    for r in range(rates.shape[0]):
        turned = turned + jnp.where(partners[r : r + 1] == label, rates[r : r + 1], 0.0)
    blank = jnp.zeros((classes, LANES - classes), jnp.float32)
    turned = jnp.concatenate([turned, blank], 1)
    full = jnp.concatenate([turned, jnp.zeros((LANES - classes, LANES), jnp.float32)], 0).T[:classes]
    low = jnp.where(square < owner, full + turned, jnp.where(square == owner, full, 0.0))
    full = full - jnp.where(owner == classes - 1, low, 0.0)
    low = jnp.where(owner > 0, roll(low, 1, 0), 0.0)
    both = jnp.concatenate([low, full], 0)
    high_part = both.astype(jnp.bfloat16).astype(jnp.float32)
    low_part = both - high_part
    column = lax.broadcasted_iota(jnp.int32, (2 * classes, LANES), 1)
    weights = jnp.where(column < classes, high_part, roll(low_part, classes, 1)).astype(jnp.bfloat16)
    flat_grown = grown.reshape(classes * rows, LANES)

    def grow(pair):
        parts = [
            flat[pl.ds(2 * pair + h, classes, stride=rows), :].astype(jnp.bfloat16) for h in range(2)
        ]
        narrow = jnp.concatenate(parts, 1)
        mixed = jnp.dot(
            weights, jnp.concatenate([narrow, narrow], 0), preferred_element_type=jnp.float32
        )
        for h in range(2):
            n = parts[h].astype(jnp.float32)
            piece = mixed[:, h * LANES : (h + 1) * LANES]
            flat_grown[pl.ds(2 * pair + h, classes, stride=rows), :] = (
                roll(n, 1, 0) * piece[:classes] - n * piece[classes:]
            )

    pl.loop(0, rows // 2, unroll=4)(grow)

    cell = lax.broadcasted_iota(jnp.int32, (rows, 1), 0)
    full_y = SIDE * wide
    base = ((me_x * SIDE + cell // SIDE) * full_y + me_y * SIDE + cell % SIDE) * LANES
    hit = [
        jnp.max(jnp.where(nozzle[...] == base + z, 1.0, 0.0), axis=1, keepdims=True) for z in range(2)
    ]
    deep = lax.broadcasted_iota(jnp.int32, (rows, LANES), 1)
    coef[8] = jnp.where(deep == 0, hit[0], jnp.where(deep == 1, hit[1], 0.0))

    arrived(0, send_a, recv_a)
    strips = [jnp.zeros((wide, LANES), jnp.float32) for _ in range(PITCH)]
    for by in range(wide):
        line = roll(recv_a[by * wide : (by + 1) * wide], SIDE * by - 1, 1)
        for slot in range(PITCH):
            strips[slot] = strips[slot] + line * masks[by * SLOTS + slot : by * SLOTS + slot + 1]
    for slot in range(SLOTS):
        send_b[pl.ds(slot, wide, stride=SLOTS), :] = (
            roll(strips[slot], turn_of(slot), 1)
            if slot < PITCH
            else jnp.zeros((wide, LANES), jnp.float32)
        )
    exchange(1, send_b, recv_b, me_x, along_x)

    for copy in moving_faces:
        copy.wait_recv()
    has_x = [(me_x > 0).astype(jnp.float32), (me_x < wide - 1).astype(jnp.float32)]
    has_y = [(me_y > 0).astype(jnp.float32), (me_y < wide - 1).astype(jnp.float32)]

    def moving_at(a, x):
        if x < 0:
            return face_x[0, classes + a] * has_x[0]
        if x >= SIDE:
            return face_x[1, classes + a] * has_x[1]
        return ext[classes + a, SIDE * x : SIDE * x + SIDE]

    def around_y(a, x):
        here = moving_at(a, x)
        below = jnp.where(row == 0, face_y[0, classes + a, x : x + 1] * has_y[0], roll(here, 1, 0))
        above = jnp.where(
            row == SIDE - 1, face_y[1, classes + a, x : x + 1] * has_y[1], roll(here, -1, 0)
        )
        return below, above

    for x in range(SIDE):
        part = slice(SIDE * x, SIDE * x + SIDE)
        stop = coef[8, part]
        scale = step_size * material[x].astype(jnp.float32) * (1.0 - stop)
        total = jnp.zeros((SIDE, LANES), jnp.float32)
        for a in range(3):
            here = moving_at(a, x)
            if a == 0:
                below, above = moving_at(0, x - 1), moving_at(0, x + 1)
            elif a == 1:
                below, above = around_y(1, x)
            else:
                below, above = down_z(here), up_z(here)
            up, down = 0.5 * (here + above), 0.5 * (below + here)
            total = total + (jnp.maximum(up, 0.0) - jnp.minimum(down, 0.0))
            plus, minus = -scale * jnp.minimum(up, 0.0), scale * jnp.maximum(down, 0.0)
            if a == 0:
                if x == 0:
                    minus = minus * has_x[0]
                if x == SIDE - 1:
                    plus = plus * has_x[1]
            elif a == 1:
                edge_y[0, x : x + 1] = minus[0:1] * has_y[0]
                edge_y[1, x : x + 1] = plus[SIDE - 1 : SIDE] * has_y[1]
                minus = jnp.where(row == 0, 0.0, minus)
                plus = jnp.where(row == SIDE - 1, 0.0, plus)
            else:
                minus = jnp.where(not_first, minus, 0.0)
                plus = jnp.where(not_last, plus, 0.0)
            coef[2 * a + 1, part] = minus
            coef[2 * a + 2, part] = plus
        coef[0, part] = 1.0 - stop - scale * total
        coef[7, part] = scale

    flat_result = result.reshape(classes * rows, LANES)

    def advance(k):
        fill = inlet[k]
        for x in range(SIDE):
            part = slice(SIDE * x, SIDE * x + SIDE)
            here = ext[k, part]
            value = (
                (coef[0, part] * here + coef[7, part] * grown[k, part])
                + (coef[3, part] * roll(here, 1, 0) + coef[4, part] * roll(here, -1, 0))
                + (coef[5, part] * roll(here, 1, 1) + coef[6, part] * roll(here, -1, 1))
                + coef[8, part] * fill
            )
            if x > 0:
                value = value + coef[1, part] * ext[k, SIDE * x - SIDE : SIDE * x]
            if x < SIDE - 1:
                value = value + coef[2, part] * ext[k, SIDE * x + SIDE : SIDE * x + 2 * SIDE]
            result[k, part] = value

    def finish(k):
        for side, start in ((0, 0), (1, rows - SIDE)):
            part = slice(start, start + SIDE)
            result[k, part] = result[k, part] + coef[1 + side, part] * face_x[side, k]
        for side in range(2):
            part = pl.ds(k * rows + side * (SIDE - 1), SIDE, stride=SIDE)
            flat_result[part, :] = flat_result[part, :] + edge_y[side] * face_y[side, k]

    pl.loop(0, classes, unroll=2)(advance)

    wave = factor_z[me_y * wide + me_x]
    inverse = -1.0 / ((factor_x[...] + wave) + factor_y[...])
    arrived(1, send_b, recv_b)
    plane = dot(dot(forward_x[...], recv_b[...]), forward_y[...]) * inverse
    send_c[...] = dot(backward_x[...], dot(plane, backward_y[...]))
    exchange(2, send_c, recv_c, me_x, along_x)
    arrived(2, send_c, recv_c)
    strips = [
        roll(recv_c[pl.ds(slot, wide, stride=SLOTS), :], -turn_of(slot), 1) for slot in range(PITCH)
    ]
    for by in range(wide):
        total = jnp.zeros((wide, LANES), jnp.float32)
        for slot in range(PITCH):
            total = total + strips[slot] * masks[by * SLOTS + slot : by * SLOTS + slot + 1]
        send_d[by * wide : (by + 1) * wide] = roll(total, 1 - SIDE * by, 1)
    exchange(3, send_d, recv_d, me_y, along_y)

    for copy in moment_faces:
        copy.wait_recv()
    pl.loop(0, classes, unroll=4)(finish)

    arrived(3, send_d, recv_d)
    poten[...] = dot(recv_d[...], inverse_z[...], ((0,), (0,)))
    for x in range(SIDE):
        part = slice(SIDE * x, SIDE * x + SIDE)

        def pot(x):
            if x < 0:
                return poten[edge : edge + SIDE]
            if x >= SIDE:
                return poten[edge + SIDE : edge + 2 * SIDE]
            return poten[PITCH * x + 1 : PITCH * x + 1 + SIDE]

        low_y = poten[PITCH * x : PITCH * x + SIDE]
        high_y = poten[PITCH * x + 2 : PITCH * x + 2 + SIDE]
        middle = pot(x)
        gradient = (
            0.5 * (pot(x + 1) - pot(x - 1)),
            0.5 * (high_y - low_y),
            0.5 * (up_z(middle) - down_z(middle)),
        )
        c = current_at(x)
        d = [c[a] - gradient[a] for a in range(3)]
        f = [field[a, x] for a in range(3)]
        lorentz = (d[1] * f[2] - d[2] * f[1], d[2] * f[0] - d[0] * f[2], d[0] * f[1] - d[1] * f[0])
        liquid = material[x].astype(jnp.float32)
        stop = coef[8, part] > 0.5
        for a in range(3):
            here = moving_at(a, x)
            below, above = around_y(a, x)
            spread = (
                (moving_at(a, x - 1) + moving_at(a, x + 1))
                + (below + above)
                + (down_z(here) + up_z(here))
                - 6.0 * here
            )
            value = liquid * (here + step_size * (lorentz[a] + viscosity * spread))
            new_velocity[a, x] = jnp.where(stop, jet[a], value)

    for phase, buffer in enumerate((send_a, send_b, send_c, send_d)):
        sent(phase, buffer)
    for copy in moving_faces + moment_faces:
        copy.wait_send()


def local(velocity, moments, field, material, nozzle, jet, inlet, rates, partners):
    width_x = lax.axis_size("gx")
    width_y = lax.axis_size("grp") * lax.axis_size("gy")
    cells_x, cells_y, depth = material.shape
    classes = moments.shape[0]
    rows = cells_x * cells_y
    table = tables(cells_x * width_x, cells_y * width_y, depth)
    f32 = jnp.float32
    operands = (
        velocity, field, material, moments.reshape(classes, rows, depth),
        nozzle.reshape(1, -1), jet, inlet, rates.T, partners.T,
        table["basis_z"], table["inverse_z"], table["forward_x"], table["backward_x"],
        table["forward_y"], table["backward_y"], table["factor_x"], table["factor_y"],
        table["factor_z"], table["masks"],
    )
    scalars = (5, 6, 17)
    here = [
        (pltpu.SMEM if number in scalars else pltpu.VMEM)(array.shape, array.dtype)
        for number, array in enumerate(operands)
        if number != 3
    ]
    vmem = pl.BlockSpec(memory_space=pltpu.VMEM)
    far = pl.BlockSpec(memory_space=pltpu.HBM)
    square = pltpu.VMEM((2 * LANES, LANES), f32)
    faces = pltpu.VMEM((2, classes + 3, SIDE, LANES), f32)
    new_velocity, new_moments = pl.pallas_call(
        kernel,
        out_shape=(
            pltpu.VMEM(velocity.shape, f32),
            pltpu.VMEM((classes, rows, depth), f32),
        ),
        in_specs=[far] * len(operands),
        out_specs=(vmem, vmem),
        scratch_shapes=here + [
            pltpu.VMEM((classes + 3, rows, LANES), f32),
            pltpu.VMEM((classes, rows, LANES), f32),
            faces, faces, faces,
            pltpu.VMEM((9, rows, LANES), f32),
            pltpu.VMEM((2, SIDE, LANES), f32),
            pltpu.VMEM((LANES, LANES), f32),
            square, square, square, square, square, square, square, square,
            pltpu.VMEM((LANES, LANES), f32),
            pltpu.SemaphoreType.DMA,
            pltpu.SemaphoreType.DMA((4,)),
            pltpu.SemaphoreType.DMA((14,)),
            pltpu.SemaphoreType.DMA((8,)),
            pltpu.SemaphoreType.DMA((8,)),
            pltpu.SemaphoreType.DMA((4,)),
            pltpu.SemaphoreType.DMA((4,)),
        ],
        compiler_params=pltpu.CompilerParams(
            collective_id=0, has_side_effects=True, vmem_limit_bytes=60 * 1024 * 1024
        ),
    )(*operands)
    return (new_velocity, new_moments.reshape(moments.shape))


def solution(mesh):
    bricks = P(None, "gx", ("grp", "gy"), None)
    return jax.shard_map(
        local,
        mesh=mesh,
        in_specs=(bricks, bricks, bricks, P("gx", ("grp", "gy"), None), P(), P(), P(), P(), P()),
        out_specs=(bricks, bricks),
        check_vma=False,
    )
```

```python
import functools
import math

import jax
import jax.numpy as jnp
import numpy as np
from jax import lax
from jax.experimental import pallas as pl
from jax.experimental.pallas import tpu as pltpu
from jax.sharding import PartitionSpec as P

step_size = 0.2
viscosity = 0.5
screening = 0.0001
MESH = pl.DeviceIdType.MESH
SIDE = 8
PITCH = 10
SLOTS = 16
CHAINS = 2
STRIDE = 24
LANES = 128


def wave_of(length):
    index = np.arange(2 * length)
    return np.where(index <= length, index, index - length)


def real_basis(length):
    span = 2 * length
    index = np.arange(span)
    angle = 2.0 * math.pi / span * ((wave_of(length)[:, None] * np.arange(length)[None, :]) % span)
    return np.where(index[:, None] <= length, np.cos(angle), np.sin(angle))


def real_weights(length):
    span = 2 * length
    weights = np.full(span, 2.0 / span)
    weights[0] = weights[length] = 1.0 / span
    return weights


def wave_factors(length):
    return 2.0 - 2.0 * np.cos(2.0 * math.pi * wave_of(length) / (2 * length))


def tables(full_x, full_y, depth):
    bricks_x, bricks_y = full_x // SIDE, full_y // SIDE
    levels = bricks_x // CHAINS
    basis_x, basis_y, basis_z = real_basis(full_x), real_basis(full_y), real_basis(depth)
    inverse_x = basis_x * real_weights(full_x)[:, None]
    inverse_y = basis_y * real_weights(full_y)[:, None]
    inverse_z = basis_z * real_weights(depth)[:, None]
    forward_x = np.zeros((2 * full_x, levels * STRIDE))
    backward_x = np.zeros((levels * STRIDE, 2 * full_x))
    for brick in range(bricks_x):
        for slot in range(PITCH):
            x = SIDE * brick + (slot if slot < SIDE else (-1 if slot == SIDE else SIDE))
            if 0 <= x < full_x:
                place = brick % levels * STRIDE + brick // levels * PITCH + slot
                forward_x[:, place] = basis_x[:, x]
                backward_x[place] = inverse_x[:, x]
    masks = np.zeros((bricks_y, SLOTS, LANES))
    for brick in range(bricks_y):
        for slot in range(PITCH):
            for lane in range(LANES):
                source = (lane - (SIDE * brick - 1)) % LANES
                if slot < SIDE:
                    y = SIDE * brick - 1 + source - PITCH * slot
                    inside = 0 <= source - PITCH * slot < PITCH
                else:
                    offset = source - PITCH * SIDE - SIDE * (slot - SIDE)
                    y = SIDE * brick + offset
                    inside = 0 <= offset < SIDE
                if inside and 0 <= y < full_y:
                    masks[brick, slot, lane] = 1.0
    f32 = lambda array: jnp.asarray(np.asarray(array, np.float32))
    return dict(
        basis_z=f32(basis_z),
        inverse_z=f32(inverse_z),
        forward_x=f32(forward_x),
        backward_x=f32(backward_x),
        forward_y=f32(basis_y.T),
        backward_y=f32(inverse_y),
        factor_x=f32(wave_factors(full_x)[:, None]),
        factor_y=f32(wave_factors(full_y)[None, :]),
        factor_z=f32(wave_factors(depth) + screening),
        masks=f32(masks.reshape(bricks_y * SLOTS, LANES)),
    )


def turn_of(slot):
    return (-PITCH * slot if slot < SIDE else 1 - PITCH * SIDE - SIDE * (slot - SIDE)) % LANES


def roll(values, shift, axis):
    shift = shift % values.shape[axis]
    return values if shift == 0 else pltpu.roll(values, shift, axis)


def dot(first, second, dims=((1,), (0,))):
    return lax.dot_general(
        first,
        second,
        (dims, ((), ())),
        precision=lax.Precision.HIGHEST,
        preferred_element_type=jnp.float32,
    )


def kernel(
    velocity_in, field_in, material_in, moments, nozzle_in, jet_in, inlet_in, rates_in, partners_in,
    basis_z_in, inverse_z_in, forward_x_in, backward_x_in, forward_y_in, backward_y_in,
    factor_x_in, factor_y_in, factor_z_in, masks_in,
    new_velocity, result,
    velocity, field, material, nozzle, jet, inlet, rates, partners,
    basis_z, inverse_z, forward_x, backward_x, forward_y, backward_y,
    factor_x, factor_y, factor_z, masks,
    ext, grown, face_x, face_y, cut_y, coef,
    edge_y, source, send_a, recv_a, send_b, recv_b, send_c, recv_c, send_d, recv_d, poten,
    load_sem, first_sem, later_sem, halo_send, halo_recv, ssem, rsem,
):
    wide = 16
    classes = rates.shape[1]
    rows = SIDE * SIDE
    me_x = lax.axis_index("gx")
    me_grp, me_gy = lax.axis_index("grp"), lax.axis_index("gy")
    groups = lax.axis_size("gy")
    me_y = me_grp * groups + me_gy
    levels = wide // CHAINS
    me_z = lax.rem(me_x, levels)
    me_sheet = me_x // levels * wide + me_y

    def along_x(index):
        return {"gx": index}

    def along_y(index):
        return {"grp": index // groups, "gy": lax.rem(index, groups)}

    def along_z(index):
        return {"gx": me_x - me_z + index}

    def in_sheet(index):
        line = lax.rem(index, wide)
        return {
            "gx": index // wide * levels + me_z,
            "grp": line // groups,
            "gy": lax.rem(line, groups),
        }

    first = [
        pltpu.make_async_copy(src, dst, first_sem.at[number])
        for number, (src, dst) in enumerate(
            [(velocity_in, velocity), (field_in, field), (material_in, material), (basis_z_in, basis_z)]
        )
    ]
    load = pltpu.make_async_copy(moments, ext.at[pl.ds(0, classes)], load_sem)
    later = [
        pltpu.make_async_copy(src, dst, later_sem.at[number])
        for number, (src, dst) in enumerate(
            [
                (nozzle_in, nozzle), (jet_in, jet), (inlet_in, inlet), (rates_in, rates),
                (partners_in, partners), (inverse_z_in, inverse_z), (forward_x_in, forward_x),
                (backward_x_in, backward_x), (forward_y_in, forward_y), (backward_y_in, backward_y),
                (factor_x_in, factor_x), (factor_y_in, factor_y), (factor_z_in, factor_z),
                (masks_in, masks),
            ]
        )
    ]
    for copy in first + [load] + later:
        copy.start()
    barrier = pltpu.get_barrier_semaphore()

    def greet(device):
        pl.semaphore_signal(barrier, inc=1, device_id=device, device_id_type=MESH)

    pl.loop(1, CHAINS * wide)(lambda k: greet(in_sheet(lax.rem(me_sheet + k, CHAINS * wide))))
    pl.loop(1, levels)(lambda k: greet(along_z(lax.rem(me_z + k, levels))))
    greet(along_x(lax.rem(me_x + 1, wide)))
    greet(along_x(lax.rem(me_x + wide - 1, wide)))

    lane = lax.broadcasted_iota(jnp.int32, (SIDE, LANES), 1)
    row = lax.broadcasted_iota(jnp.int32, (SIDE, LANES), 0)
    not_first, not_last = lane != 0, lane != LANES - 1

    def up_z(v):
        return jnp.where(not_last, roll(v, -1, 1), 0.0)

    def down_z(v):
        return jnp.where(not_first, roll(v, 1, 1), 0.0)

    def current_at(x):
        m = [ext[classes + a, SIDE * x : SIDE * x + SIDE] for a in range(3)]
        f = [field[a, x] for a in range(3)]
        return (
            m[1] * f[2] - m[2] * f[1],
            m[2] * f[0] - m[0] * f[2],
            m[0] * f[1] - m[1] * f[0],
        )

    for copy in first:
        copy.wait()

    for x in range(SIDE):
        liquid = material[x].astype(jnp.float32)
        for a in range(3):
            ext[classes + a, SIDE * x : SIDE * x + SIDE] = velocity[a, x] * liquid
    currents = [current_at(x) for x in range(SIDE)]
    for x in range(SIDE):
        c1, c2 = currents[x][1], currents[x][2]
        s = jnp.where(row < SIDE - 1, roll(c1, -1, 0), 0.0) - jnp.where(row > 0, roll(c1, 1, 0), 0.0)
        s = s + up_z(c2) - down_z(c2)
        if x + 1 < SIDE:
            s = s + currents[x + 1][0]
        if x > 0:
            s = s - currents[x - 1][0]
        source[PITCH * x + 1 : PITCH * x + 1 + SIDE] = 0.5 * s
        source[PITCH * x : PITCH * x + 1] = 0.5 * c1[0:1]
        source[PITCH * x + PITCH - 1 : PITCH * x + PITCH] = -0.5 * c1[SIDE - 1 : SIDE]
    edge = PITCH * SIDE
    source[edge : edge + SIDE] = 0.5 * currents[0][0]
    source[edge + SIDE : edge + 2 * SIDE] = -0.5 * currents[SIDE - 1][0]
    source[edge + 2 * SIDE :] = jnp.zeros((LANES - edge - 2 * SIDE, LANES), jnp.float32)
    send_a[...] = dot(basis_z[...], source[...], ((1,), (1,)))

    pl.semaphore_wait(barrier, CHAINS * wide + levels)

    def exchange(phase, send, recv, me, target, count, size):
        mine = pl.ds(pl.multiple_of(me * size, size), size)

        def start(step):
            other = lax.rem(me + step, count)
            pltpu.make_async_remote_copy(
                src_ref=send.at[pl.ds(pl.multiple_of(other * size, size), size)],
                dst_ref=recv.at[mine],
                send_sem=ssem.at[phase],
                recv_sem=rsem.at[phase],
                device_id=target(other),
                device_id_type=MESH,
            ).start()

        pl.loop(1, count)(start)
        recv[mine] = send[mine]

    def arrived(phase, recv, count, size):
        part = pl.ds(0, (count - 1) * size)
        pltpu.make_async_copy(recv.at[part], recv.at[part], rsem.at[phase]).wait()

    def sent(phase, send, count, size):
        part = pl.ds(0, (count - 1) * size)
        pltpu.make_async_copy(send.at[part], send.at[part], ssem.at[phase]).wait()

    sheet, column = (CHAINS * wide, SIDE), (levels, STRIDE)

    flat = ext.reshape((classes + 3) * rows, LANES)
    lower_x, upper_x = lax.rem(me_x + wide - 1, wide), lax.rem(me_x + 1, wide)
    lower_y, upper_y = lax.rem(me_y + wide - 1, wide), lax.rem(me_y + 1, wide)

    moment_faces = []

    def send_faces(copies, along, begin, count):
        part = pl.ds(begin, count)
        if along == "y":
            for side in range(2):
                cut_y[side, part] = flat[
                    pl.ds(begin * rows + side * (SIDE - 1), count * SIDE, stride=SIDE), :
                ].reshape(count, SIDE, LANES)
            jobs = (
                (cut_y.at[0, part], face_y.at[1, part], along_y(lower_y)),
                (cut_y.at[1, part], face_y.at[0, part], along_y(upper_y)),
            )
        else:
            jobs = (
                (ext.at[part, pl.ds(0, SIDE)], face_x.at[1, part], along_x(lower_x)),
                (ext.at[part, pl.ds(rows - SIDE, SIDE)], face_x.at[0, part], along_x(upper_x)),
            )
        for src, dst, device in jobs:
            number = len(moving_faces) + len(moment_faces)
            copy = pltpu.make_async_remote_copy(
                src_ref=src,
                dst_ref=dst,
                send_sem=halo_send.at[number],
                recv_sem=halo_recv.at[number],
                device_id=device,
                device_id_type=MESH,
            )
            copy.start()
            copies.append(copy)

    moving_faces = []
    exchange(0, send_a, recv_a, me_sheet, in_sheet, *sheet)
    send_faces(moving_faces, "y", classes, 3)
    send_faces(moving_faces, "x", classes, 3)
    load.wait()
    send_faces(moment_faces, "x", 0, 32)
    for copy in later:
        copy.wait()

    square = lax.broadcasted_iota(jnp.int32, (classes, LANES), 1)
    owner = lax.broadcasted_iota(jnp.int32, (classes, LANES), 0)
    label = lax.broadcasted_iota(jnp.int32, (classes, classes), 0)
    turned = jnp.zeros((classes, classes), jnp.float32)
    for r in range(rates.shape[0]):
        turned = turned + jnp.where(partners[r : r + 1] == label, rates[r : r + 1], 0.0)
    blank = jnp.zeros((classes, LANES - classes), jnp.float32)
    turned = jnp.concatenate([turned, blank], 1)
    full = jnp.concatenate([turned, jnp.zeros((LANES - classes, LANES), jnp.float32)], 0).T[:classes]
    low = jnp.where(square < owner, full + turned, jnp.where(square == owner, full, 0.0))
    full = full - jnp.where(owner == classes - 1, low, 0.0)
    low = jnp.where(owner > 0, roll(low, 1, 0), 0.0)
    both = jnp.concatenate([low, full], 0)
    high_part = both.astype(jnp.bfloat16).astype(jnp.float32)
    low_part = both - high_part
    place = lax.broadcasted_iota(jnp.int32, (2 * classes, LANES), 1)
    weights = jnp.where(place < classes, high_part, roll(low_part, classes, 1)).astype(jnp.bfloat16)
    flat_grown = grown.reshape(classes * rows, LANES)

    def grow(pair):
        parts = [
            flat[pl.ds(2 * pair + h, classes, stride=rows), :].astype(jnp.bfloat16) for h in range(2)
        ]
        narrow = jnp.concatenate(parts, 1)
        mixed = jnp.dot(
            weights, jnp.concatenate([narrow, narrow], 0), preferred_element_type=jnp.float32
        )
        for h in range(2):
            n = parts[h].astype(jnp.float32)
            piece = mixed[:, h * LANES : (h + 1) * LANES]
            flat_grown[pl.ds(2 * pair + h, classes, stride=rows), :] = (
                roll(n, 1, 0) * piece[:classes] - n * piece[classes:]
            )

    pl.loop(0, rows // 2, unroll=4)(grow)

    cell = lax.broadcasted_iota(jnp.int32, (rows, 1), 0)
    full_y = SIDE * wide
    base = ((me_x * SIDE + cell // SIDE) * full_y + me_y * SIDE + cell % SIDE) * LANES
    hit = [
        jnp.max(jnp.where(nozzle[...] == base + z, 1.0, 0.0), axis=1, keepdims=True) for z in range(2)
    ]
    deep = lax.broadcasted_iota(jnp.int32, (rows, LANES), 1)
    coef[8] = jnp.where(deep == 0, hit[0], jnp.where(deep == 1, hit[1], 0.0))

    arrived(0, recv_a, *sheet)
    for chain in range(CHAINS):
        strips = [jnp.zeros((levels, LANES), jnp.float32) for _ in range(PITCH)]
        for by in range(wide):
            place = (chain * wide + by) * SIDE
            line = roll(recv_a[place : place + SIDE], SIDE * by - 1, 1)
            for slot in range(PITCH):
                strips[slot] = strips[slot] + line * masks[by * SLOTS + slot : by * SLOTS + slot + 1]
        for slot in range(PITCH):
            send_b[pl.ds(chain * PITCH + slot, levels, stride=STRIDE), :] = roll(
                strips[slot], turn_of(slot), 1
            )
    for slot in range(CHAINS * PITCH, STRIDE):
        send_b[pl.ds(slot, levels, stride=STRIDE), :] = jnp.zeros((levels, LANES), jnp.float32)
    exchange(1, send_b, recv_b, me_z, along_z, *column)
    send_faces(moment_faces, "y", 0, 32)

    for copy in moving_faces:
        copy.wait_recv()
    has_x = [(me_x > 0).astype(jnp.float32), (me_x < wide - 1).astype(jnp.float32)]
    has_y = [(me_y > 0).astype(jnp.float32), (me_y < wide - 1).astype(jnp.float32)]

    def moving_at(a, x):
        if x < 0:
            return face_x[0, classes + a] * has_x[0]
        if x >= SIDE:
            return face_x[1, classes + a] * has_x[1]
        return ext[classes + a, SIDE * x : SIDE * x + SIDE]

    def around_y(a, x):
        here = moving_at(a, x)
        below = jnp.where(row == 0, face_y[0, classes + a, x : x + 1] * has_y[0], roll(here, 1, 0))
        above = jnp.where(
            row == SIDE - 1, face_y[1, classes + a, x : x + 1] * has_y[1], roll(here, -1, 0)
        )
        return below, above

    for x in range(SIDE):
        part = slice(SIDE * x, SIDE * x + SIDE)
        stop = coef[8, part]
        scale = step_size * material[x].astype(jnp.float32) * (1.0 - stop)
        total = jnp.zeros((SIDE, LANES), jnp.float32)
        for a in range(3):
            here = moving_at(a, x)
            if a == 0:
                below, above = moving_at(0, x - 1), moving_at(0, x + 1)
            elif a == 1:
                below, above = around_y(1, x)
            else:
                below, above = down_z(here), up_z(here)
            up, down = 0.5 * (here + above), 0.5 * (below + here)
            total = total + (jnp.maximum(up, 0.0) - jnp.minimum(down, 0.0))
            plus, minus = -scale * jnp.minimum(up, 0.0), scale * jnp.maximum(down, 0.0)
            if a == 0:
                if x == 0:
                    minus = minus * has_x[0]
                if x == SIDE - 1:
                    plus = plus * has_x[1]
            elif a == 1:
                edge_y[0, x : x + 1] = minus[0:1] * has_y[0]
                edge_y[1, x : x + 1] = plus[SIDE - 1 : SIDE] * has_y[1]
                minus = jnp.where(row == 0, 0.0, minus)
                plus = jnp.where(row == SIDE - 1, 0.0, plus)
            else:
                minus = jnp.where(not_first, minus, 0.0)
                plus = jnp.where(not_last, plus, 0.0)
            coef[2 * a + 1, part] = minus
            coef[2 * a + 2, part] = plus
        coef[0, part] = 1.0 - stop - scale * total
        coef[7, part] = scale

    flat_result = result.reshape(classes * rows, LANES)

    def advance(k):
        fill = inlet[k]
        for x in range(SIDE):
            part = slice(SIDE * x, SIDE * x + SIDE)
            here = ext[k, part]
            value = (
                (coef[0, part] * here + coef[7, part] * grown[k, part])
                + (coef[3, part] * roll(here, 1, 0) + coef[4, part] * roll(here, -1, 0))
                + (coef[5, part] * roll(here, 1, 1) + coef[6, part] * roll(here, -1, 1))
                + coef[8, part] * fill
            )
            if x > 0:
                value = value + coef[1, part] * ext[k, SIDE * x - SIDE : SIDE * x]
            if x < SIDE - 1:
                value = value + coef[2, part] * ext[k, SIDE * x + SIDE : SIDE * x + 2 * SIDE]
            result[k, part] = value

    def finish(k):
        for side, start in ((0, 0), (1, rows - SIDE)):
            part = slice(start, start + SIDE)
            result[k, part] = result[k, part] + coef[1 + side, part] * face_x[side, k]
        for side in range(2):
            part = pl.ds(k * rows + side * (SIDE - 1), SIDE, stride=SIDE)
            flat_result[part, :] = flat_result[part, :] + edge_y[side] * face_y[side, k]

    pl.loop(0, classes, unroll=2)(advance)

    wave = factor_z[me_sheet * levels + me_z]
    inverse = -1.0 / ((factor_x[...] + wave) + factor_y[...])
    arrived(1, recv_b, *column)
    plane = dot(dot(forward_x[...], recv_b[...]), forward_y[...]) * inverse
    send_c[...] = dot(backward_x[...], dot(plane, backward_y[...]))
    exchange(2, send_c, recv_c, me_z, along_z, *column)
    send_faces(moment_faces, "y", 32, 32)
    arrived(2, recv_c, *column)
    for chain in range(CHAINS):
        strips = [
            roll(recv_c[pl.ds(chain * PITCH + slot, levels, stride=STRIDE), :], -turn_of(slot), 1)
            for slot in range(PITCH)
        ]
        for by in range(wide):
            total = jnp.zeros((levels, LANES), jnp.float32)
            for slot in range(PITCH):
                total = total + strips[slot] * masks[by * SLOTS + slot : by * SLOTS + slot + 1]
            place = (chain * wide + by) * SIDE
            send_d[place : place + SIDE] = roll(total, 1 - SIDE * by, 1)
    exchange(3, send_d, recv_d, me_sheet, in_sheet, *sheet)
    send_faces(moment_faces, "x", 32, 32)

    for copy in moment_faces:
        copy.wait_recv()
    pl.loop(0, classes, unroll=4)(finish)

    arrived(3, recv_d, *sheet)
    poten[...] = dot(recv_d[...], inverse_z[...], ((0,), (0,)))
    for x in range(SIDE):
        part = slice(SIDE * x, SIDE * x + SIDE)

        def pot(x):
            if x < 0:
                return poten[edge : edge + SIDE]
            if x >= SIDE:
                return poten[edge + SIDE : edge + 2 * SIDE]
            return poten[PITCH * x + 1 : PITCH * x + 1 + SIDE]

        low_y = poten[PITCH * x : PITCH * x + SIDE]
        high_y = poten[PITCH * x + 2 : PITCH * x + 2 + SIDE]
        middle = pot(x)
        gradient = (
            0.5 * (pot(x + 1) - pot(x - 1)),
            0.5 * (high_y - low_y),
            0.5 * (up_z(middle) - down_z(middle)),
        )
        c = current_at(x)
        d = [c[a] - gradient[a] for a in range(3)]
        f = [field[a, x] for a in range(3)]
        lorentz = (d[1] * f[2] - d[2] * f[1], d[2] * f[0] - d[0] * f[2], d[0] * f[1] - d[1] * f[0])
        liquid = material[x].astype(jnp.float32)
        stop = coef[8, part] > 0.5
        for a in range(3):
            here = moving_at(a, x)
            below, above = around_y(a, x)
            spread = (
                (moving_at(a, x - 1) + moving_at(a, x + 1))
                + (below + above)
                + (down_z(here) + up_z(here))
                - 6.0 * here
            )
            value = liquid * (here + step_size * (lorentz[a] + viscosity * spread))
            new_velocity[a, x] = jnp.where(stop, jet[a], value)

    for phase, buffer, shape in (
        (0, send_a, sheet), (1, send_b, column), (2, send_c, column), (3, send_d, sheet),
    ):
        sent(phase, buffer, *shape)
    for copy in moving_faces + moment_faces:
        copy.wait_send()


def local(velocity, moments, field, material, nozzle, jet, inlet, rates, partners):
    width_x = lax.axis_size("gx")
    width_y = lax.axis_size("grp") * lax.axis_size("gy")
    cells_x, cells_y, depth = material.shape
    classes = moments.shape[0]
    rows = cells_x * cells_y
    table = tables(cells_x * width_x, cells_y * width_y, depth)
    f32 = jnp.float32
    operands = (
        velocity, field, material, moments.reshape(classes, rows, depth),
        nozzle.reshape(1, -1), jet, inlet, rates.T, partners.T,
        table["basis_z"], table["inverse_z"], table["forward_x"], table["backward_x"],
        table["forward_y"], table["backward_y"], table["factor_x"], table["factor_y"],
        table["factor_z"], table["masks"],
    )
    scalars = (5, 6, 17)
    here = [
        (pltpu.SMEM if number in scalars else pltpu.VMEM)(array.shape, array.dtype)
        for number, array in enumerate(operands)
        if number != 3
    ]
    vmem = pl.BlockSpec(memory_space=pltpu.VMEM)
    far = pl.BlockSpec(memory_space=pltpu.HBM)
    square = pltpu.VMEM((2 * LANES, LANES), f32)
    narrow = pltpu.VMEM((width_x // CHAINS * STRIDE, LANES), f32)
    faces = pltpu.VMEM((2, classes + 3, SIDE, LANES), f32)
    new_velocity, new_moments = pl.pallas_call(
        kernel,
        out_shape=(
            pltpu.VMEM(velocity.shape, f32),
            pltpu.VMEM((classes, rows, depth), f32),
        ),
        in_specs=[far] * len(operands),
        out_specs=(vmem, vmem),
        scratch_shapes=here + [
            pltpu.VMEM((classes + 3, rows, LANES), f32),
            pltpu.VMEM((classes, rows, LANES), f32),
            faces, faces, faces,
            pltpu.VMEM((9, rows, LANES), f32),
            pltpu.VMEM((2, SIDE, LANES), f32),
            pltpu.VMEM((LANES, LANES), f32),
            square, square, narrow, narrow, narrow, narrow, square, square,
            pltpu.VMEM((LANES, LANES), f32),
            pltpu.SemaphoreType.DMA,
            pltpu.SemaphoreType.DMA((4,)),
            pltpu.SemaphoreType.DMA((14,)),
            pltpu.SemaphoreType.DMA((16,)),
            pltpu.SemaphoreType.DMA((16,)),
            pltpu.SemaphoreType.DMA((4,)),
            pltpu.SemaphoreType.DMA((4,)),
        ],
        compiler_params=pltpu.CompilerParams(
            collective_id=0, has_side_effects=True, vmem_limit_bytes=60 * 1024 * 1024
        ),
    )(*operands)
    return (new_velocity, new_moments.reshape(moments.shape))


def solution(mesh):
    bricks = P(None, "gx", ("grp", "gy"), None)
    return jax.shard_map(
        local,
        mesh=mesh,
        in_specs=(bricks, bricks, bricks, P("gx", ("grp", "gy"), None), P(), P(), P(), P(), P()),
        out_specs=(bricks, bricks),
        check_vma=False,
    )
```

```python
import functools
import math

import jax
import jax.numpy as jnp
import numpy as np
from jax import lax
from jax.experimental import pallas as pl
from jax.experimental.pallas import tpu as pltpu
from jax.sharding import PartitionSpec as P

step_size = 0.2
viscosity = 0.5
screening = 0.0001
MESH = pl.DeviceIdType.MESH
SIDE = 8
PITCH = 10
SLOTS = 16
CHAINS = 2
STRIDE = 24
LANES = 128


def wave_of(length):
    index = np.arange(2 * length)
    return np.where(index <= length, index, index - length)


def real_basis(length):
    span = 2 * length
    index = np.arange(span)
    angle = 2.0 * math.pi / span * ((wave_of(length)[:, None] * np.arange(length)[None, :]) % span)
    return np.where(index[:, None] <= length, np.cos(angle), np.sin(angle))


def real_weights(length):
    span = 2 * length
    weights = np.full(span, 2.0 / span)
    weights[0] = weights[length] = 1.0 / span
    return weights


def wave_factors(length):
    return 2.0 - 2.0 * np.cos(2.0 * math.pi * wave_of(length) / (2 * length))


def tables(full_x, full_y, depth):
    bricks_x, bricks_y = full_x // SIDE, full_y // SIDE
    levels = bricks_x // CHAINS
    basis_x, basis_y, basis_z = real_basis(full_x), real_basis(full_y), real_basis(depth)
    inverse_x = basis_x * real_weights(full_x)[:, None]
    inverse_y = basis_y * real_weights(full_y)[:, None]
    inverse_z = basis_z * real_weights(depth)[:, None]
    forward_x = np.zeros((2 * full_x, levels * STRIDE))
    backward_x = np.zeros((levels * STRIDE, 2 * full_x))
    for brick in range(bricks_x):
        for slot in range(PITCH):
            x = SIDE * brick + (slot if slot < SIDE else (-1 if slot == SIDE else SIDE))
            if 0 <= x < full_x:
                place = brick % levels * STRIDE + brick // levels * PITCH + slot
                forward_x[:, place] = basis_x[:, x]
                backward_x[place] = inverse_x[:, x]
    masks = np.zeros((bricks_y, SLOTS, LANES))
    for brick in range(bricks_y):
        for slot in range(PITCH):
            for lane in range(LANES):
                source = (lane - (SIDE * brick - 1)) % LANES
                if slot < SIDE:
                    y = SIDE * brick - 1 + source - PITCH * slot
                    inside = 0 <= source - PITCH * slot < PITCH
                else:
                    offset = source - PITCH * SIDE - SIDE * (slot - SIDE)
                    y = SIDE * brick + offset
                    inside = 0 <= offset < SIDE
                if inside and 0 <= y < full_y:
                    masks[brick, slot, lane] = 1.0
    f32 = lambda array: jnp.asarray(np.asarray(array, np.float32))
    return dict(
        basis_z=f32(basis_z),
        inverse_z=f32(inverse_z),
        forward_x=f32(forward_x),
        backward_x=f32(backward_x),
        forward_y=f32(basis_y.T),
        backward_y=f32(inverse_y),
        factor_x=f32(wave_factors(full_x)[:, None]),
        factor_y=f32(wave_factors(full_y)[None, :]),
        factor_z=f32(wave_factors(depth) + screening),
        masks=f32(masks.reshape(bricks_y * SLOTS, LANES)),
    )


def turn_of(slot):
    return (-PITCH * slot if slot < SIDE else 1 - PITCH * SIDE - SIDE * (slot - SIDE)) % LANES


def roll(values, shift, axis):
    shift = shift % values.shape[axis]
    return values if shift == 0 else pltpu.roll(values, shift, axis)


def dot(first, second, dims=((1,), (0,))):
    return lax.dot_general(
        first,
        second,
        (dims, ((), ())),
        precision=lax.Precision.HIGH,
        preferred_element_type=jnp.float32,
    )


def kernel(
    velocity_in, field_in, material_in, moments, nozzle_in, jet_in, inlet_in, rates_in, partners_in,
    basis_z_in, inverse_z_in, forward_x_in, backward_x_in, forward_y_in, backward_y_in,
    factor_x_in, factor_y_in, factor_z_in, masks_in,
    new_velocity, result,
    velocity, field, material, nozzle, jet, inlet, rates, partners,
    basis_z, inverse_z, forward_x, backward_x, forward_y, backward_y,
    factor_x, factor_y, factor_z, masks,
    ext, grown, face_x, face_y, cut_y, coef,
    edge_y, source, send_a, recv_a, send_b, recv_b, send_c, recv_c, send_d, recv_d, poten,
    load_sem, first_sem, later_sem, halo_send, halo_recv, ssem, rsem,
):
    wide = 16
    classes = rates.shape[1]
    rows = SIDE * SIDE
    me_x = lax.axis_index("gx")
    me_grp, me_gy = lax.axis_index("grp"), lax.axis_index("gy")
    groups = lax.axis_size("gy")
    me_y = me_grp * groups + me_gy
    levels = wide // CHAINS
    me_z = lax.rem(me_x, levels)
    me_sheet = me_x // levels * wide + me_y

    def along_x(index):
        return {"gx": index}

    def along_y(index):
        return {"grp": index // groups, "gy": lax.rem(index, groups)}

    def along_z(index):
        return {"gx": me_x - me_z + index}

    def in_sheet(index):
        line = lax.rem(index, wide)
        return {
            "gx": index // wide * levels + me_z,
            "grp": line // groups,
            "gy": lax.rem(line, groups),
        }

    first = [
        pltpu.make_async_copy(src, dst, first_sem.at[number])
        for number, (src, dst) in enumerate(
            [(velocity_in, velocity), (field_in, field), (material_in, material), (basis_z_in, basis_z)]
        )
    ]
    load = pltpu.make_async_copy(moments, ext.at[pl.ds(0, classes)], load_sem)
    later = [
        pltpu.make_async_copy(src, dst, later_sem.at[number])
        for number, (src, dst) in enumerate(
            [
                (nozzle_in, nozzle), (jet_in, jet), (inlet_in, inlet), (rates_in, rates),
                (partners_in, partners), (inverse_z_in, inverse_z), (forward_x_in, forward_x),
                (backward_x_in, backward_x), (forward_y_in, forward_y), (backward_y_in, backward_y),
                (factor_x_in, factor_x), (factor_y_in, factor_y), (factor_z_in, factor_z),
                (masks_in, masks),
            ]
        )
    ]
    for copy in first + [load] + later:
        copy.start()
    barrier = pltpu.get_barrier_semaphore()

    def greet(device):
        pl.semaphore_signal(barrier, inc=1, device_id=device, device_id_type=MESH)

    pl.loop(1, CHAINS * wide)(lambda k: greet(in_sheet(lax.rem(me_sheet + k, CHAINS * wide))))
    pl.loop(1, levels)(lambda k: greet(along_z(lax.rem(me_z + k, levels))))
    greet(along_x(lax.rem(me_x + 1, wide)))
    greet(along_x(lax.rem(me_x + wide - 1, wide)))

    lane = lax.broadcasted_iota(jnp.int32, (SIDE, LANES), 1)
    row = lax.broadcasted_iota(jnp.int32, (SIDE, LANES), 0)
    not_first, not_last = lane != 0, lane != LANES - 1

    def up_z(v):
        return jnp.where(not_last, roll(v, -1, 1), 0.0)

    def down_z(v):
        return jnp.where(not_first, roll(v, 1, 1), 0.0)

    def current_at(x):
        m = [ext[classes + a, SIDE * x : SIDE * x + SIDE] for a in range(3)]
        f = [field[a, x] for a in range(3)]
        return (
            m[1] * f[2] - m[2] * f[1],
            m[2] * f[0] - m[0] * f[2],
            m[0] * f[1] - m[1] * f[0],
        )

    for copy in first:
        copy.wait()

    for x in range(SIDE):
        liquid = material[x].astype(jnp.float32)
        for a in range(3):
            ext[classes + a, SIDE * x : SIDE * x + SIDE] = velocity[a, x] * liquid
    currents = [current_at(x) for x in range(SIDE)]
    for x in range(SIDE):
        c1, c2 = currents[x][1], currents[x][2]
        s = jnp.where(row < SIDE - 1, roll(c1, -1, 0), 0.0) - jnp.where(row > 0, roll(c1, 1, 0), 0.0)
        s = s + up_z(c2) - down_z(c2)
        if x + 1 < SIDE:
            s = s + currents[x + 1][0]
        if x > 0:
            s = s - currents[x - 1][0]
        source[PITCH * x + 1 : PITCH * x + 1 + SIDE] = 0.5 * s
        source[PITCH * x : PITCH * x + 1] = 0.5 * c1[0:1]
        source[PITCH * x + PITCH - 1 : PITCH * x + PITCH] = -0.5 * c1[SIDE - 1 : SIDE]
    edge = PITCH * SIDE
    source[edge : edge + SIDE] = 0.5 * currents[0][0]
    source[edge + SIDE : edge + 2 * SIDE] = -0.5 * currents[SIDE - 1][0]
    source[edge + 2 * SIDE :] = jnp.zeros((LANES - edge - 2 * SIDE, LANES), jnp.float32)
    send_a[...] = dot(basis_z[...], source[...], ((1,), (1,)))

    pl.semaphore_wait(barrier, CHAINS * wide + levels)

    def exchange(phase, send, recv, me, target, count, size):
        mine = pl.ds(pl.multiple_of(me * size, size), size)

        def start(step):
            other = lax.rem(me + step, count)
            pltpu.make_async_remote_copy(
                src_ref=send.at[pl.ds(pl.multiple_of(other * size, size), size)],
                dst_ref=recv.at[mine],
                send_sem=ssem.at[phase],
                recv_sem=rsem.at[phase],
                device_id=target(other),
                device_id_type=MESH,
            ).start()

        pl.loop(1, count)(start)
        recv[mine] = send[mine]

    def arrived(phase, recv, count, size):
        part = pl.ds(0, (count - 1) * size)
        pltpu.make_async_copy(recv.at[part], recv.at[part], rsem.at[phase]).wait()

    def sent(phase, send, count, size):
        part = pl.ds(0, (count - 1) * size)
        pltpu.make_async_copy(send.at[part], send.at[part], ssem.at[phase]).wait()

    sheet, column = (CHAINS * wide, SIDE), (levels, STRIDE)

    flat = ext.reshape((classes + 3) * rows, LANES)
    lower_x, upper_x = lax.rem(me_x + wide - 1, wide), lax.rem(me_x + 1, wide)
    lower_y, upper_y = lax.rem(me_y + wide - 1, wide), lax.rem(me_y + 1, wide)

    moment_faces = []

    def send_faces(copies, along, begin, count):
        part = pl.ds(begin, count)
        if along == "y":
            for side in range(2):
                cut_y[side, part] = flat[
                    pl.ds(begin * rows + side * (SIDE - 1), count * SIDE, stride=SIDE), :
                ].reshape(count, SIDE, LANES)
            jobs = (
                (cut_y.at[0, part], face_y.at[1, part], along_y(lower_y)),
                (cut_y.at[1, part], face_y.at[0, part], along_y(upper_y)),
            )
        else:
            jobs = (
                (ext.at[part, pl.ds(0, SIDE)], face_x.at[1, part], along_x(lower_x)),
                (ext.at[part, pl.ds(rows - SIDE, SIDE)], face_x.at[0, part], along_x(upper_x)),
            )
        for src, dst, device in jobs:
            number = len(moving_faces) + len(moment_faces)
            copy = pltpu.make_async_remote_copy(
                src_ref=src,
                dst_ref=dst,
                send_sem=halo_send.at[number],
                recv_sem=halo_recv.at[number],
                device_id=device,
                device_id_type=MESH,
            )
            copy.start()
            copies.append(copy)

    moving_faces = []
    exchange(0, send_a, recv_a, me_sheet, in_sheet, *sheet)
    send_faces(moving_faces, "y", classes, 3)
    send_faces(moving_faces, "x", classes, 3)
    load.wait()
    send_faces(moment_faces, "x", 0, 32)
    for copy in later:
        copy.wait()

    square = lax.broadcasted_iota(jnp.int32, (classes, LANES), 1)
    owner = lax.broadcasted_iota(jnp.int32, (classes, LANES), 0)
    label = lax.broadcasted_iota(jnp.int32, (classes, classes), 0)
    turned = jnp.zeros((classes, classes), jnp.float32)
    for r in range(rates.shape[0]):
        turned = turned + jnp.where(partners[r : r + 1] == label, rates[r : r + 1], 0.0)
    blank = jnp.zeros((classes, LANES - classes), jnp.float32)
    turned = jnp.concatenate([turned, blank], 1)
    full = jnp.concatenate([turned, jnp.zeros((LANES - classes, LANES), jnp.float32)], 0).T[:classes]
    low = jnp.where(square < owner, full + turned, jnp.where(square == owner, full, 0.0))
    full = full - jnp.where(owner == classes - 1, low, 0.0)
    low = jnp.where(owner > 0, roll(low, 1, 0), 0.0)
    both = jnp.concatenate([low, full], 0)
    high_part = both.astype(jnp.bfloat16).astype(jnp.float32)
    low_part = both - high_part
    place = lax.broadcasted_iota(jnp.int32, (2 * classes, LANES), 1)
    weights = jnp.where(place < classes, high_part, roll(low_part, classes, 1)).astype(jnp.bfloat16)
    flat_grown = grown.reshape(classes * rows, LANES)

    def grow(pair):
        parts = [
            flat[pl.ds(2 * pair + h, classes, stride=rows), :].astype(jnp.bfloat16) for h in range(2)
        ]
        narrow = jnp.concatenate(parts, 1)
        mixed = jnp.dot(
            weights, jnp.concatenate([narrow, narrow], 0), preferred_element_type=jnp.float32
        )
        for h in range(2):
            n = parts[h].astype(jnp.float32)
            piece = mixed[:, h * LANES : (h + 1) * LANES]
            flat_grown[pl.ds(2 * pair + h, classes, stride=rows), :] = (
                roll(n, 1, 0) * piece[:classes] - n * piece[classes:]
            )

    pl.loop(0, rows // 2, unroll=4)(grow)

    cell = lax.broadcasted_iota(jnp.int32, (rows, 1), 0)
    full_y = SIDE * wide
    base = ((me_x * SIDE + cell // SIDE) * full_y + me_y * SIDE + cell % SIDE) * LANES
    hit = [
        jnp.max(jnp.where(nozzle[...] == base + z, 1.0, 0.0), axis=1, keepdims=True) for z in range(2)
    ]
    deep = lax.broadcasted_iota(jnp.int32, (rows, LANES), 1)
    coef[8] = jnp.where(deep == 0, hit[0], jnp.where(deep == 1, hit[1], 0.0))

    arrived(0, recv_a, *sheet)
    for chain in range(CHAINS):
        strips = [jnp.zeros((levels, LANES), jnp.float32) for _ in range(PITCH)]
        for by in range(wide):
            place = (chain * wide + by) * SIDE
            line = roll(recv_a[place : place + SIDE], SIDE * by - 1, 1)
            for slot in range(PITCH):
                strips[slot] = strips[slot] + line * masks[by * SLOTS + slot : by * SLOTS + slot + 1]
        for slot in range(PITCH):
            send_b[pl.ds(chain * PITCH + slot, levels, stride=STRIDE), :] = roll(
                strips[slot], turn_of(slot), 1
            )
    for slot in range(CHAINS * PITCH, STRIDE):
        send_b[pl.ds(slot, levels, stride=STRIDE), :] = jnp.zeros((levels, LANES), jnp.float32)
    exchange(1, send_b, recv_b, me_z, along_z, *column)
    send_faces(moment_faces, "y", 0, 32)

    for copy in moving_faces:
        copy.wait_recv()
    has_x = [(me_x > 0).astype(jnp.float32), (me_x < wide - 1).astype(jnp.float32)]
    has_y = [(me_y > 0).astype(jnp.float32), (me_y < wide - 1).astype(jnp.float32)]

    def moving_at(a, x):
        if x < 0:
            return face_x[0, classes + a] * has_x[0]
        if x >= SIDE:
            return face_x[1, classes + a] * has_x[1]
        return ext[classes + a, SIDE * x : SIDE * x + SIDE]

    def around_y(a, x):
        here = moving_at(a, x)
        below = jnp.where(row == 0, face_y[0, classes + a, x : x + 1] * has_y[0], roll(here, 1, 0))
        above = jnp.where(
            row == SIDE - 1, face_y[1, classes + a, x : x + 1] * has_y[1], roll(here, -1, 0)
        )
        return below, above

    for x in range(SIDE):
        part = slice(SIDE * x, SIDE * x + SIDE)
        stop = coef[8, part]
        scale = step_size * material[x].astype(jnp.float32) * (1.0 - stop)
        total = jnp.zeros((SIDE, LANES), jnp.float32)
        for a in range(3):
            here = moving_at(a, x)
            if a == 0:
                below, above = moving_at(0, x - 1), moving_at(0, x + 1)
            elif a == 1:
                below, above = around_y(1, x)
            else:
                below, above = down_z(here), up_z(here)
            up, down = 0.5 * (here + above), 0.5 * (below + here)
            total = total + (jnp.maximum(up, 0.0) - jnp.minimum(down, 0.0))
            plus, minus = -scale * jnp.minimum(up, 0.0), scale * jnp.maximum(down, 0.0)
            if a == 0:
                if x == 0:
                    minus = minus * has_x[0]
                if x == SIDE - 1:
                    plus = plus * has_x[1]
            elif a == 1:
                edge_y[0, x : x + 1] = minus[0:1] * has_y[0]
                edge_y[1, x : x + 1] = plus[SIDE - 1 : SIDE] * has_y[1]
                minus = jnp.where(row == 0, 0.0, minus)
                plus = jnp.where(row == SIDE - 1, 0.0, plus)
            else:
                minus = jnp.where(not_first, minus, 0.0)
                plus = jnp.where(not_last, plus, 0.0)
            coef[2 * a + 1, part] = minus
            coef[2 * a + 2, part] = plus
        coef[0, part] = 1.0 - stop - scale * total
        coef[7, part] = scale

    flat_result = result.reshape(classes * rows, LANES)

    def advance(k):
        fill = inlet[k]
        for x in range(SIDE):
            part = slice(SIDE * x, SIDE * x + SIDE)
            here = ext[k, part]
            value = (
                (coef[0, part] * here + coef[7, part] * grown[k, part])
                + (coef[3, part] * roll(here, 1, 0) + coef[4, part] * roll(here, -1, 0))
                + (coef[5, part] * roll(here, 1, 1) + coef[6, part] * roll(here, -1, 1))
                + coef[8, part] * fill
            )
            if x > 0:
                value = value + coef[1, part] * ext[k, SIDE * x - SIDE : SIDE * x]
            if x < SIDE - 1:
                value = value + coef[2, part] * ext[k, SIDE * x + SIDE : SIDE * x + 2 * SIDE]
            result[k, part] = value

    def finish_x(k):
        for side, start in ((0, 0), (1, rows - SIDE)):
            part = slice(start, start + SIDE)
            result[k, part] = result[k, part] + coef[1 + side, part] * face_x[side, k]

    def finish_y(k):
        for side in range(2):
            part = pl.ds(k * rows + side * (SIDE - 1), SIDE, stride=SIDE)
            flat_result[part, :] = flat_result[part, :] + edge_y[side] * face_y[side, k]

    pl.loop(0, classes, unroll=2)(advance)

    wave = factor_z[me_sheet * levels + me_z]
    inverse = -1.0 / ((factor_x[...] + wave) + factor_y[...])
    arrived(1, recv_b, *column)
    plane = dot(dot(forward_x[...], recv_b[...]), forward_y[...]) * inverse
    send_c[...] = dot(backward_x[...], dot(plane, backward_y[...]))
    exchange(2, send_c, recv_c, me_z, along_z, *column)
    send_faces(moment_faces, "y", 32, 32)
    for x in range(SIDE):
        part = slice(SIDE * x, SIDE * x + SIDE)
        c = current_at(x)
        f = [field[a, x] for a in range(3)]
        lorentz = (c[1] * f[2] - c[2] * f[1], c[2] * f[0] - c[0] * f[2], c[0] * f[1] - c[1] * f[0])
        liquid = material[x].astype(jnp.float32)
        stop = coef[8, part] > 0.5
        for a in range(3):
            here = moving_at(a, x)
            below, above = around_y(a, x)
            spread = (
                (moving_at(a, x - 1) + moving_at(a, x + 1))
                + (below + above)
                + (down_z(here) + up_z(here))
                - 6.0 * here
            )
            value = liquid * (here + step_size * (lorentz[a] + viscosity * spread))
            new_velocity[a, x] = jnp.where(stop, jet[a], value)

    arrived(2, recv_c, *column)
    for chain in range(CHAINS):
        strips = [
            roll(recv_c[pl.ds(chain * PITCH + slot, levels, stride=STRIDE), :], -turn_of(slot), 1)
            for slot in range(PITCH)
        ]
        for by in range(wide):
            total = jnp.zeros((levels, LANES), jnp.float32)
            for slot in range(PITCH):
                total = total + strips[slot] * masks[by * SLOTS + slot : by * SLOTS + slot + 1]
            place = (chain * wide + by) * SIDE
            send_d[place : place + SIDE] = roll(total, 1 - SIDE * by, 1)
    exchange(3, send_d, recv_d, me_sheet, in_sheet, *sheet)
    send_faces(moment_faces, "x", 32, 32)

    for copy in moment_faces[:4]:
        copy.wait_recv()
    pl.loop(0, classes // 2, unroll=4)(finish_x)
    pl.loop(0, classes // 2, unroll=4)(finish_y)
    for copy in moment_faces[4:6]:
        copy.wait_recv()
    pl.loop(classes // 2, classes, unroll=4)(finish_y)

    arrived(3, recv_d, *sheet)
    poten[...] = dot(recv_d[...], inverse_z[...], ((0,), (0,)))
    for x in range(SIDE):
        part = slice(SIDE * x, SIDE * x + SIDE)

        def pot(x):
            if x < 0:
                return poten[edge : edge + SIDE]
            if x >= SIDE:
                return poten[edge + SIDE : edge + 2 * SIDE]
            return poten[PITCH * x + 1 : PITCH * x + 1 + SIDE]

        low_y = poten[PITCH * x : PITCH * x + SIDE]
        high_y = poten[PITCH * x + 2 : PITCH * x + 2 + SIDE]
        middle = pot(x)
        gradient = (
            0.5 * (pot(x + 1) - pot(x - 1)),
            0.5 * (high_y - low_y),
            0.5 * (up_z(middle) - down_z(middle)),
        )
        f = [field[a, x] for a in range(3)]
        pull = (
            gradient[1] * f[2] - gradient[2] * f[1],
            gradient[2] * f[0] - gradient[0] * f[2],
            gradient[0] * f[1] - gradient[1] * f[0],
        )
        for a in range(3):
            new_velocity[a, x] = new_velocity[a, x] - coef[7, part] * pull[a]

    for copy in moment_faces[6:]:
        copy.wait_recv()
    pl.loop(classes // 2, classes, unroll=4)(finish_x)

    for phase, buffer, shape in (
        (0, send_a, sheet), (1, send_b, column), (2, send_c, column), (3, send_d, sheet),
    ):
        sent(phase, buffer, *shape)
    for copy in moving_faces + moment_faces:
        copy.wait_send()


def local(velocity, moments, field, material, nozzle, jet, inlet, rates, partners):
    width_x = lax.axis_size("gx")
    width_y = lax.axis_size("grp") * lax.axis_size("gy")
    cells_x, cells_y, depth = material.shape
    classes = moments.shape[0]
    rows = cells_x * cells_y
    table = tables(cells_x * width_x, cells_y * width_y, depth)
    f32 = jnp.float32
    operands = (
        velocity, field, material, moments.reshape(classes, rows, depth),
        nozzle.reshape(1, -1), jet, inlet, rates.T, partners.T,
        table["basis_z"], table["inverse_z"], table["forward_x"], table["backward_x"],
        table["forward_y"], table["backward_y"], table["factor_x"], table["factor_y"],
        table["factor_z"], table["masks"],
    )
    scalars = (5, 6, 17)
    here = [
        (pltpu.SMEM if number in scalars else pltpu.VMEM)(array.shape, array.dtype)
        for number, array in enumerate(operands)
        if number != 3
    ]
    vmem = pl.BlockSpec(memory_space=pltpu.VMEM)
    far = pl.BlockSpec(memory_space=pltpu.HBM)
    square = pltpu.VMEM((2 * LANES, LANES), f32)
    narrow = pltpu.VMEM((width_x // CHAINS * STRIDE, LANES), f32)
    faces = pltpu.VMEM((2, classes + 3, SIDE, LANES), f32)
    new_velocity, new_moments = pl.pallas_call(
        kernel,
        out_shape=(
            pltpu.VMEM(velocity.shape, f32),
            pltpu.VMEM((classes, rows, depth), f32),
        ),
        in_specs=[far] * len(operands),
        out_specs=(vmem, vmem),
        scratch_shapes=here + [
            pltpu.VMEM((classes + 3, rows, LANES), f32),
            pltpu.VMEM((classes, rows, LANES), f32),
            faces, faces, faces,
            pltpu.VMEM((9, rows, LANES), f32),
            pltpu.VMEM((2, SIDE, LANES), f32),
            pltpu.VMEM((LANES, LANES), f32),
            square, square, narrow, narrow, narrow, narrow, square, square,
            pltpu.VMEM((LANES, LANES), f32),
            pltpu.SemaphoreType.DMA,
            pltpu.SemaphoreType.DMA((4,)),
            pltpu.SemaphoreType.DMA((14,)),
            pltpu.SemaphoreType.DMA((16,)),
            pltpu.SemaphoreType.DMA((16,)),
            pltpu.SemaphoreType.DMA((4,)),
            pltpu.SemaphoreType.DMA((4,)),
        ],
        compiler_params=pltpu.CompilerParams(
            collective_id=0, has_side_effects=True, vmem_limit_bytes=60 * 1024 * 1024
        ),
    )(*operands)
    return (new_velocity, new_moments.reshape(moments.shape))


def solution(mesh):
    bricks = P(None, "gx", ("grp", "gy"), None)
    return jax.shard_map(
        local,
        mesh=mesh,
        in_specs=(bricks, bricks, bricks, P("gx", ("grp", "gy"), None), P(), P(), P(), P(), P()),
        out_specs=(bricks, bricks),
        check_vma=False,
    )
```

```python
import functools
import math

import jax
import jax.numpy as jnp
import numpy as np
from jax import lax
from jax.experimental import pallas as pl
from jax.experimental.pallas import tpu as pltpu
from jax.sharding import PartitionSpec as P

step_size = 0.2
viscosity = 0.5
screening = 0.0001
MESH = pl.DeviceIdType.MESH
SIDE = 8
PITCH = 10
SLOTS = 16
CHAINS = 2
STRIDE = 24
LANES = 128


def wave_of(length):
    index = np.arange(2 * length)
    return np.where(index <= length, index, index - length)


def real_basis(length):
    span = 2 * length
    index = np.arange(span)
    angle = 2.0 * math.pi / span * ((wave_of(length)[:, None] * np.arange(length)[None, :]) % span)
    return np.where(index[:, None] <= length, np.cos(angle), np.sin(angle))


def real_weights(length):
    span = 2 * length
    weights = np.full(span, 2.0 / span)
    weights[0] = weights[length] = 1.0 / span
    return weights


def wave_factors(length):
    return 2.0 - 2.0 * np.cos(2.0 * math.pi * wave_of(length) / (2 * length))


def tables(full_x, full_y, depth):
    bricks_x, bricks_y = full_x // SIDE, full_y // SIDE
    levels = bricks_x // CHAINS
    basis_x, basis_y, basis_z = real_basis(full_x), real_basis(full_y), real_basis(depth)
    inverse_x = basis_x * real_weights(full_x)[:, None]
    inverse_y = basis_y * real_weights(full_y)[:, None]
    inverse_z = basis_z * real_weights(depth)[:, None]
    forward_x = np.zeros((2 * full_x, levels * STRIDE))
    backward_x = np.zeros((levels * STRIDE, 2 * full_x))
    for brick in range(bricks_x):
        for slot in range(PITCH):
            x = SIDE * brick + (slot if slot < SIDE else (-1 if slot == SIDE else SIDE))
            if 0 <= x < full_x:
                place = brick % levels * STRIDE + brick // levels * PITCH + slot
                forward_x[:, place] = basis_x[:, x]
                backward_x[place] = inverse_x[:, x]
    masks = np.zeros((bricks_y, SLOTS, LANES))
    for brick in range(bricks_y):
        for slot in range(PITCH):
            for lane in range(LANES):
                source = (lane - (SIDE * brick - 1)) % LANES
                if slot < SIDE:
                    y = SIDE * brick - 1 + source - PITCH * slot
                    inside = 0 <= source - PITCH * slot < PITCH
                else:
                    offset = source - PITCH * SIDE - SIDE * (slot - SIDE)
                    y = SIDE * brick + offset
                    inside = 0 <= offset < SIDE
                if inside and 0 <= y < full_y:
                    masks[brick, slot, lane] = 1.0
    f32 = lambda array: jnp.asarray(np.asarray(array, np.float32))
    return dict(
        basis_z=f32(basis_z),
        inverse_z=f32(inverse_z),
        forward_x=f32(forward_x),
        backward_x=f32(backward_x),
        forward_y=f32(basis_y.T),
        backward_y=f32(inverse_y),
        factor_x=f32(wave_factors(full_x)[:, None]),
        factor_y=f32(wave_factors(full_y)[None, :]),
        factor_z=f32(wave_factors(depth) + screening),
        masks=f32(masks.reshape(bricks_y * SLOTS, LANES)),
    )


def turn_of(slot):
    return (-PITCH * slot if slot < SIDE else 1 - PITCH * SIDE - SIDE * (slot - SIDE)) % LANES


def roll(values, shift, axis):
    shift = shift % values.shape[axis]
    return values if shift == 0 else pltpu.roll(values, shift, axis)


def dot(first, second, dims=((1,), (0,))):
    return lax.dot_general(
        first,
        second,
        (dims, ((), ())),
        precision=lax.Precision.HIGH,
        preferred_element_type=jnp.float32,
    )


def kernel(
    velocity_in, field_in, material_in, moments, nozzle_in, jet_in, inlet_in, rates_in, partners_in,
    basis_z_in, inverse_z_in, forward_x_in, backward_x_in, forward_y_in, backward_y_in,
    factor_x_in, factor_y_in, factor_z_in, masks_in,
    new_velocity, result,
    velocity, field, material, nozzle, jet, inlet, rates, partners,
    basis_z, inverse_z, forward_x, backward_x, forward_y, backward_y,
    factor_x, factor_y, factor_z, masks,
    ext, grown, face_x, face_y, cut_y, coef,
    edge_y, source, send_a, recv_a, send_b, recv_b, send_c, recv_c, send_d, recv_d, poten,
    load_sem, first_sem, later_sem, halo_send, halo_recv, ssem, rsem,
):
    wide = 16
    classes = rates.shape[1]
    rows = SIDE * SIDE
    me_x = lax.axis_index("gx")
    me_grp, me_gy = lax.axis_index("grp"), lax.axis_index("gy")
    groups = lax.axis_size("gy")
    me_y = me_grp * groups + me_gy
    levels = wide // CHAINS
    me_z = lax.rem(me_x, levels)
    me_sheet = me_x // levels * wide + me_y

    def along_x(index):
        return {"gx": index}

    def along_y(index):
        return {"grp": index // groups, "gy": lax.rem(index, groups)}

    def along_z(index):
        return {"gx": me_x - me_z + index}

    def in_sheet(index):
        line = lax.rem(index, wide)
        return {
            "gx": index // wide * levels + me_z,
            "grp": line // groups,
            "gy": lax.rem(line, groups),
        }

    first = [
        pltpu.make_async_copy(src, dst, first_sem.at[number])
        for number, (src, dst) in enumerate(
            [(velocity_in, velocity), (field_in, field), (material_in, material), (basis_z_in, basis_z)]
        )
    ]
    load = pltpu.make_async_copy(moments, ext.at[pl.ds(0, classes)], load_sem)
    later = [
        pltpu.make_async_copy(src, dst, later_sem.at[number])
        for number, (src, dst) in enumerate(
            [
                (nozzle_in, nozzle), (jet_in, jet), (inlet_in, inlet), (rates_in, rates),
                (partners_in, partners), (inverse_z_in, inverse_z), (forward_x_in, forward_x),
                (backward_x_in, backward_x), (forward_y_in, forward_y), (backward_y_in, backward_y),
                (factor_x_in, factor_x), (factor_y_in, factor_y), (factor_z_in, factor_z),
                (masks_in, masks),
            ]
        )
    ]
    for copy in first + [load] + later:
        copy.start()
    barrier = pltpu.get_barrier_semaphore()

    def greet(device):
        pl.semaphore_signal(barrier, inc=1, device_id=device, device_id_type=MESH)

    pl.loop(1, CHAINS * wide)(lambda k: greet(in_sheet(lax.rem(me_sheet + k, CHAINS * wide))))
    pl.loop(1, levels)(lambda k: greet(along_z(lax.rem(me_z + k, levels))))
    greet(along_x(lax.rem(me_x + 1, wide)))
    greet(along_x(lax.rem(me_x + wide - 1, wide)))

    lane = lax.broadcasted_iota(jnp.int32, (SIDE, LANES), 1)
    row = lax.broadcasted_iota(jnp.int32, (SIDE, LANES), 0)
    not_first, not_last = lane != 0, lane != LANES - 1

    def up_z(v):
        return jnp.where(not_last, roll(v, -1, 1), 0.0)

    def down_z(v):
        return jnp.where(not_first, roll(v, 1, 1), 0.0)

    def current_at(x):
        m = [ext[classes + a, SIDE * x : SIDE * x + SIDE] for a in range(3)]
        f = [field[a, x] for a in range(3)]
        return (
            m[1] * f[2] - m[2] * f[1],
            m[2] * f[0] - m[0] * f[2],
            m[0] * f[1] - m[1] * f[0],
        )

    for copy in first:
        copy.wait()

    for x in range(SIDE):
        liquid = material[x].astype(jnp.float32)
        for a in range(3):
            ext[classes + a, SIDE * x : SIDE * x + SIDE] = velocity[a, x] * liquid
    currents = [current_at(x) for x in range(SIDE)]
    for x in range(SIDE):
        c1, c2 = currents[x][1], currents[x][2]
        s = jnp.where(row < SIDE - 1, roll(c1, -1, 0), 0.0) - jnp.where(row > 0, roll(c1, 1, 0), 0.0)
        s = s + up_z(c2) - down_z(c2)
        if x + 1 < SIDE:
            s = s + currents[x + 1][0]
        if x > 0:
            s = s - currents[x - 1][0]
        source[PITCH * x + 1 : PITCH * x + 1 + SIDE] = 0.5 * s
        source[PITCH * x : PITCH * x + 1] = 0.5 * c1[0:1]
        source[PITCH * x + PITCH - 1 : PITCH * x + PITCH] = -0.5 * c1[SIDE - 1 : SIDE]
    edge = PITCH * SIDE
    source[edge : edge + SIDE] = 0.5 * currents[0][0]
    source[edge + SIDE : edge + 2 * SIDE] = -0.5 * currents[SIDE - 1][0]
    source[edge + 2 * SIDE :] = jnp.zeros((LANES - edge - 2 * SIDE, LANES), jnp.float32)
    send_a[...] = dot(basis_z[...], source[...], ((1,), (1,)))

    pl.semaphore_wait(barrier, CHAINS * wide + levels)

    def exchange(phase, send, recv, me, target, count, size):
        mine = pl.ds(pl.multiple_of(me * size, size), size)

        def start(step):
            other = lax.rem(me + step, count)
            pltpu.make_async_remote_copy(
                src_ref=send.at[pl.ds(pl.multiple_of(other * size, size), size)],
                dst_ref=recv.at[mine],
                send_sem=ssem.at[phase],
                recv_sem=rsem.at[phase],
                device_id=target(other),
                device_id_type=MESH,
            ).start()

        pl.loop(1, count)(start)
        recv[mine] = send[mine]

    def arrived(phase, recv, count, size):
        part = pl.ds(0, (count - 1) * size)
        pltpu.make_async_copy(recv.at[part], recv.at[part], rsem.at[phase]).wait()

    def sent(phase, send, count, size):
        part = pl.ds(0, (count - 1) * size)
        pltpu.make_async_copy(send.at[part], send.at[part], ssem.at[phase]).wait()

    sheet, column = (CHAINS * wide, SIDE), (levels, STRIDE)

    flat = ext.reshape((classes + 3) * rows, LANES)
    lower_x, upper_x = lax.rem(me_x + wide - 1, wide), lax.rem(me_x + 1, wide)
    lower_y, upper_y = lax.rem(me_y + wide - 1, wide), lax.rem(me_y + 1, wide)

    moment_faces = []

    def send_faces(copies, along, begin, count):
        part = pl.ds(begin, count)
        if along == "y":
            for side in range(2):
                cut_y[side, part] = flat[
                    pl.ds(begin * rows + side * (SIDE - 1), count * SIDE, stride=SIDE), :
                ].reshape(count, SIDE, LANES)
            jobs = (
                (cut_y.at[0, part], face_y.at[1, part], along_y(lower_y)),
                (cut_y.at[1, part], face_y.at[0, part], along_y(upper_y)),
            )
        else:
            jobs = (
                (ext.at[part, pl.ds(0, SIDE)], face_x.at[1, part], along_x(lower_x)),
                (ext.at[part, pl.ds(rows - SIDE, SIDE)], face_x.at[0, part], along_x(upper_x)),
            )
        for src, dst, device in jobs:
            number = len(moving_faces) + len(moment_faces)
            copy = pltpu.make_async_remote_copy(
                src_ref=src,
                dst_ref=dst,
                send_sem=halo_send.at[number],
                recv_sem=halo_recv.at[number],
                device_id=device,
                device_id_type=MESH,
            )
            copy.start()
            copies.append(copy)

    moving_faces = []
    exchange(0, send_a, recv_a, me_sheet, in_sheet, *sheet)
    send_faces(moving_faces, "y", classes, 3)
    send_faces(moving_faces, "x", classes, 3)
    load.wait()
    for copy in later:
        copy.wait()

    square = lax.broadcasted_iota(jnp.int32, (classes, LANES), 1)
    owner = lax.broadcasted_iota(jnp.int32, (classes, LANES), 0)
    label = lax.broadcasted_iota(jnp.int32, (classes, classes), 0)
    turned = jnp.zeros((classes, classes), jnp.float32)
    for r in range(rates.shape[0]):
        turned = turned + jnp.where(partners[r : r + 1] == label, rates[r : r + 1], 0.0)
    blank = jnp.zeros((classes, LANES - classes), jnp.float32)
    turned = jnp.concatenate([turned, blank], 1)
    full = jnp.concatenate([turned, jnp.zeros((LANES - classes, LANES), jnp.float32)], 0).T[:classes]
    low = jnp.where(square < owner, full + turned, jnp.where(square == owner, full, 0.0))
    full = full - jnp.where(owner == classes - 1, low, 0.0)
    low = jnp.where(owner > 0, roll(low, 1, 0), 0.0)
    both = jnp.concatenate([low, full], 0)
    high_part = both.astype(jnp.bfloat16).astype(jnp.float32)
    low_part = both - high_part
    place = lax.broadcasted_iota(jnp.int32, (2 * classes, LANES), 1)
    weights = jnp.where(place < classes, high_part, roll(low_part, classes, 1)).astype(jnp.bfloat16)
    flat_grown = grown.reshape(classes * rows, LANES)

    def grow(pair):
        parts = [
            flat[pl.ds(2 * pair + h, classes, stride=rows), :].astype(jnp.bfloat16) for h in range(2)
        ]
        narrow = jnp.concatenate(parts, 1)
        mixed = jnp.dot(
            weights, jnp.concatenate([narrow, narrow], 0), preferred_element_type=jnp.float32
        )
        for h in range(2):
            n = parts[h].astype(jnp.float32)
            piece = mixed[:, h * LANES : (h + 1) * LANES]
            flat_grown[pl.ds(2 * pair + h, classes, stride=rows), :] = (
                roll(n, 1, 0) * piece[:classes] - n * piece[classes:]
            )

    pl.loop(0, rows // 4, unroll=4)(grow)
    send_faces(moment_faces, "x", 0, 32)
    pl.loop(rows // 4, rows // 2, unroll=4)(grow)

    cell = lax.broadcasted_iota(jnp.int32, (rows, 1), 0)
    full_y = SIDE * wide
    base = ((me_x * SIDE + cell // SIDE) * full_y + me_y * SIDE + cell % SIDE) * LANES
    hit = [
        jnp.max(jnp.where(nozzle[...] == base + z, 1.0, 0.0), axis=1, keepdims=True) for z in range(2)
    ]
    deep = lax.broadcasted_iota(jnp.int32, (rows, LANES), 1)
    coef[8] = jnp.where(deep == 0, hit[0], jnp.where(deep == 1, hit[1], 0.0))

    arrived(0, recv_a, *sheet)
    for chain in range(CHAINS):
        strips = [jnp.zeros((levels, LANES), jnp.float32) for _ in range(PITCH)]
        for by in range(wide):
            place = (chain * wide + by) * SIDE
            line = roll(recv_a[place : place + SIDE], SIDE * by - 1, 1)
            for slot in range(PITCH):
                strips[slot] = strips[slot] + line * masks[by * SLOTS + slot : by * SLOTS + slot + 1]
        for slot in range(PITCH):
            send_b[pl.ds(chain * PITCH + slot, levels, stride=STRIDE), :] = roll(
                strips[slot], turn_of(slot), 1
            )
    for slot in range(CHAINS * PITCH, STRIDE):
        send_b[pl.ds(slot, levels, stride=STRIDE), :] = jnp.zeros((levels, LANES), jnp.float32)
    exchange(1, send_b, recv_b, me_z, along_z, *column)
    send_faces(moment_faces, "y", 0, 32)

    for copy in moving_faces:
        copy.wait_recv()
    has_x = [(me_x > 0).astype(jnp.float32), (me_x < wide - 1).astype(jnp.float32)]
    has_y = [(me_y > 0).astype(jnp.float32), (me_y < wide - 1).astype(jnp.float32)]

    def moving_at(a, x):
        if x < 0:
            return face_x[0, classes + a] * has_x[0]
        if x >= SIDE:
            return face_x[1, classes + a] * has_x[1]
        return ext[classes + a, SIDE * x : SIDE * x + SIDE]

    def around_y(a, x):
        here = moving_at(a, x)
        below = jnp.where(row == 0, face_y[0, classes + a, x : x + 1] * has_y[0], roll(here, 1, 0))
        above = jnp.where(
            row == SIDE - 1, face_y[1, classes + a, x : x + 1] * has_y[1], roll(here, -1, 0)
        )
        return below, above

    for x in range(SIDE):
        part = slice(SIDE * x, SIDE * x + SIDE)
        stop = coef[8, part]
        scale = step_size * material[x].astype(jnp.float32) * (1.0 - stop)
        total = jnp.zeros((SIDE, LANES), jnp.float32)
        for a in range(3):
            here = moving_at(a, x)
            if a == 0:
                below, above = moving_at(0, x - 1), moving_at(0, x + 1)
            elif a == 1:
                below, above = around_y(1, x)
            else:
                below, above = down_z(here), up_z(here)
            up, down = 0.5 * (here + above), 0.5 * (below + here)
            total = total + (jnp.maximum(up, 0.0) - jnp.minimum(down, 0.0))
            plus, minus = -scale * jnp.minimum(up, 0.0), scale * jnp.maximum(down, 0.0)
            if a == 0:
                if x == 0:
                    minus = minus * has_x[0]
                if x == SIDE - 1:
                    plus = plus * has_x[1]
            elif a == 1:
                edge_y[0, x : x + 1] = minus[0:1] * has_y[0]
                edge_y[1, x : x + 1] = plus[SIDE - 1 : SIDE] * has_y[1]
                minus = jnp.where(row == 0, 0.0, minus)
                plus = jnp.where(row == SIDE - 1, 0.0, plus)
            else:
                minus = jnp.where(not_first, minus, 0.0)
                plus = jnp.where(not_last, plus, 0.0)
            coef[2 * a + 1, part] = minus
            coef[2 * a + 2, part] = plus
        coef[0, part] = 1.0 - stop - scale * total
        coef[7, part] = scale

    flat_result = result.reshape(classes * rows, LANES)

    def advance(k):
        fill = inlet[k]
        for x in range(SIDE):
            part = slice(SIDE * x, SIDE * x + SIDE)
            here = ext[k, part]
            value = (
                (coef[0, part] * here + coef[7, part] * grown[k, part])
                + (coef[3, part] * roll(here, 1, 0) + coef[4, part] * roll(here, -1, 0))
                + (coef[5, part] * roll(here, 1, 1) + coef[6, part] * roll(here, -1, 1))
                + coef[8, part] * fill
            )
            if x > 0:
                value = value + coef[1, part] * ext[k, SIDE * x - SIDE : SIDE * x]
            if x < SIDE - 1:
                value = value + coef[2, part] * ext[k, SIDE * x + SIDE : SIDE * x + 2 * SIDE]
            result[k, part] = value

    def finish_x(k):
        for side, start in ((0, 0), (1, rows - SIDE)):
            part = slice(start, start + SIDE)
            result[k, part] = result[k, part] + coef[1 + side, part] * face_x[side, k]

    def finish_y(k):
        for side in range(2):
            part = pl.ds(k * rows + side * (SIDE - 1), SIDE, stride=SIDE)
            flat_result[part, :] = flat_result[part, :] + edge_y[side] * face_y[side, k]

    pl.loop(0, classes, unroll=2)(advance)

    wave = factor_z[me_sheet * levels + me_z]
    inverse = -1.0 / ((factor_x[...] + wave) + factor_y[...])
    arrived(1, recv_b, *column)
    plane = dot(dot(forward_x[...], recv_b[...]), forward_y[...]) * inverse
    send_c[...] = dot(backward_x[...], dot(plane, backward_y[...]))
    exchange(2, send_c, recv_c, me_z, along_z, *column)
    send_faces(moment_faces, "y", 32, 32)
    for x in range(SIDE):
        part = slice(SIDE * x, SIDE * x + SIDE)
        c = current_at(x)
        f = [field[a, x] for a in range(3)]
        lorentz = (c[1] * f[2] - c[2] * f[1], c[2] * f[0] - c[0] * f[2], c[0] * f[1] - c[1] * f[0])
        liquid = material[x].astype(jnp.float32)
        stop = coef[8, part] > 0.5
        for a in range(3):
            here = moving_at(a, x)
            below, above = around_y(a, x)
            spread = (
                (moving_at(a, x - 1) + moving_at(a, x + 1))
                + (below + above)
                + (down_z(here) + up_z(here))
                - 6.0 * here
            )
            value = liquid * (here + step_size * (lorentz[a] + viscosity * spread))
            new_velocity[a, x] = jnp.where(stop, jet[a], value)

    arrived(2, recv_c, *column)
    for chain in range(CHAINS):
        strips = [
            roll(recv_c[pl.ds(chain * PITCH + slot, levels, stride=STRIDE), :], -turn_of(slot), 1)
            for slot in range(PITCH)
        ]
        for by in range(wide):
            total = jnp.zeros((levels, LANES), jnp.float32)
            for slot in range(PITCH):
                total = total + strips[slot] * masks[by * SLOTS + slot : by * SLOTS + slot + 1]
            place = (chain * wide + by) * SIDE
            send_d[place : place + SIDE] = roll(total, 1 - SIDE * by, 1)
    exchange(3, send_d, recv_d, me_sheet, in_sheet, *sheet)
    send_faces(moment_faces, "x", 32, 32)

    for copy in moment_faces[:4]:
        copy.wait_recv()
    pl.loop(0, classes // 2, unroll=4)(finish_x)
    pl.loop(0, classes // 2, unroll=4)(finish_y)
    for copy in moment_faces[4:6]:
        copy.wait_recv()
    pl.loop(classes // 2, classes, unroll=4)(finish_y)

    arrived(3, recv_d, *sheet)
    poten[...] = dot(recv_d[...], inverse_z[...], ((0,), (0,)))
    for x in range(SIDE):
        part = slice(SIDE * x, SIDE * x + SIDE)

        def pot(x):
            if x < 0:
                return poten[edge : edge + SIDE]
            if x >= SIDE:
                return poten[edge + SIDE : edge + 2 * SIDE]
            return poten[PITCH * x + 1 : PITCH * x + 1 + SIDE]

        low_y = poten[PITCH * x : PITCH * x + SIDE]
        high_y = poten[PITCH * x + 2 : PITCH * x + 2 + SIDE]
        middle = pot(x)
        gradient = (
            0.5 * (pot(x + 1) - pot(x - 1)),
            0.5 * (high_y - low_y),
            0.5 * (up_z(middle) - down_z(middle)),
        )
        f = [field[a, x] for a in range(3)]
        pull = (
            gradient[1] * f[2] - gradient[2] * f[1],
            gradient[2] * f[0] - gradient[0] * f[2],
            gradient[0] * f[1] - gradient[1] * f[0],
        )
        for a in range(3):
            new_velocity[a, x] = new_velocity[a, x] - coef[7, part] * pull[a]

    for copy in moment_faces[6:]:
        copy.wait_recv()
    pl.loop(classes // 2, classes, unroll=4)(finish_x)

    for phase, buffer, shape in (
        (0, send_a, sheet), (1, send_b, column), (2, send_c, column), (3, send_d, sheet),
    ):
        sent(phase, buffer, *shape)
    for copy in moving_faces + moment_faces:
        copy.wait_send()


def local(velocity, moments, field, material, nozzle, jet, inlet, rates, partners):
    width_x = lax.axis_size("gx")
    width_y = lax.axis_size("grp") * lax.axis_size("gy")
    cells_x, cells_y, depth = material.shape
    classes = moments.shape[0]
    rows = cells_x * cells_y
    table = tables(cells_x * width_x, cells_y * width_y, depth)
    f32 = jnp.float32
    operands = (
        velocity, field, material, moments.reshape(classes, rows, depth),
        nozzle.reshape(1, -1), jet, inlet, rates.T, partners.T,
        table["basis_z"], table["inverse_z"], table["forward_x"], table["backward_x"],
        table["forward_y"], table["backward_y"], table["factor_x"], table["factor_y"],
        table["factor_z"], table["masks"],
    )
    scalars = (5, 6, 17)
    here = [
        (pltpu.SMEM if number in scalars else pltpu.VMEM)(array.shape, array.dtype)
        for number, array in enumerate(operands)
        if number != 3
    ]
    vmem = pl.BlockSpec(memory_space=pltpu.VMEM)
    far = pl.BlockSpec(memory_space=pltpu.HBM)
    square = pltpu.VMEM((2 * LANES, LANES), f32)
    narrow = pltpu.VMEM((width_x // CHAINS * STRIDE, LANES), f32)
    faces = pltpu.VMEM((2, classes + 3, SIDE, LANES), f32)
    new_velocity, new_moments = pl.pallas_call(
        kernel,
        out_shape=(
            pltpu.VMEM(velocity.shape, f32),
            pltpu.VMEM((classes, rows, depth), f32),
        ),
        in_specs=[far] * len(operands),
        out_specs=(vmem, vmem),
        scratch_shapes=here + [
            pltpu.VMEM((classes + 3, rows, LANES), f32),
            pltpu.VMEM((classes, rows, LANES), f32),
            faces, faces, faces,
            pltpu.VMEM((9, rows, LANES), f32),
            pltpu.VMEM((2, SIDE, LANES), f32),
            pltpu.VMEM((LANES, LANES), f32),
            square, square, narrow, narrow, narrow, narrow, square, square,
            pltpu.VMEM((LANES, LANES), f32),
            pltpu.SemaphoreType.DMA,
            pltpu.SemaphoreType.DMA((4,)),
            pltpu.SemaphoreType.DMA((14,)),
            pltpu.SemaphoreType.DMA((16,)),
            pltpu.SemaphoreType.DMA((16,)),
            pltpu.SemaphoreType.DMA((4,)),
            pltpu.SemaphoreType.DMA((4,)),
        ],
        compiler_params=pltpu.CompilerParams(
            collective_id=0, has_side_effects=True, vmem_limit_bytes=60 * 1024 * 1024
        ),
    )(*operands)
    return (new_velocity, new_moments.reshape(moments.shape))


def solution(mesh):
    bricks = P(None, "gx", ("grp", "gy"), None)
    return jax.shard_map(
        local,
        mesh=mesh,
        in_specs=(bricks, bricks, bricks, P("gx", ("grp", "gy"), None), P(), P(), P(), P(), P()),
        out_specs=(bricks, bricks),
        check_vma=False,
    )
```

```python
import functools
import math

import jax
import jax.numpy as jnp
import numpy as np
from jax import lax
from jax.experimental import pallas as pl
from jax.experimental.pallas import tpu as pltpu
from jax.sharding import PartitionSpec as P

step_size = 0.2
viscosity = 0.5
screening = 0.0001
MESH = pl.DeviceIdType.MESH
SIDE = 8
PITCH = 10
SLOTS = 16
CHAINS = 2
STRIDE = 24
LANES = 128


def wave_of(length):
    index = np.arange(2 * length)
    return np.where(index <= length, index, index - length)


def real_basis(length):
    span = 2 * length
    index = np.arange(span)
    angle = 2.0 * math.pi / span * ((wave_of(length)[:, None] * np.arange(length)[None, :]) % span)
    return np.where(index[:, None] <= length, np.cos(angle), np.sin(angle))


def real_weights(length):
    span = 2 * length
    weights = np.full(span, 2.0 / span)
    weights[0] = weights[length] = 1.0 / span
    return weights


def wave_factors(length):
    return 2.0 - 2.0 * np.cos(2.0 * math.pi * wave_of(length) / (2 * length))


def tables(full_x, full_y, depth):
    bricks_x, bricks_y = full_x // SIDE, full_y // SIDE
    levels = bricks_x // CHAINS
    basis_x, basis_y, basis_z = real_basis(full_x), real_basis(full_y), real_basis(depth)
    inverse_x = basis_x * real_weights(full_x)[:, None]
    inverse_y = basis_y * real_weights(full_y)[:, None]
    inverse_z = basis_z * real_weights(depth)[:, None]
    forward_x = np.zeros((2 * full_x, levels * STRIDE))
    backward_x = np.zeros((levels * STRIDE, 2 * full_x))
    for brick in range(bricks_x):
        for slot in range(PITCH):
            x = SIDE * brick + (slot if slot < SIDE else (-1 if slot == SIDE else SIDE))
            if 0 <= x < full_x:
                place = brick % levels * STRIDE + brick // levels * PITCH + slot
                forward_x[:, place] = basis_x[:, x]
                backward_x[place] = inverse_x[:, x]
    masks = np.zeros((bricks_y, SLOTS, LANES))
    for brick in range(bricks_y):
        for slot in range(PITCH):
            for lane in range(LANES):
                source = (lane - (SIDE * brick - 1)) % LANES
                if slot < SIDE:
                    y = SIDE * brick - 1 + source - PITCH * slot
                    inside = 0 <= source - PITCH * slot < PITCH
                else:
                    offset = source - PITCH * SIDE - SIDE * (slot - SIDE)
                    y = SIDE * brick + offset
                    inside = 0 <= offset < SIDE
                if inside and 0 <= y < full_y:
                    masks[brick, slot, lane] = 1.0
    f32 = lambda array: jnp.asarray(np.asarray(array, np.float32))
    return dict(
        basis_z=f32(basis_z),
        inverse_z=f32(inverse_z),
        forward_x=f32(forward_x),
        backward_x=f32(backward_x),
        forward_y=f32(basis_y.T),
        backward_y=f32(inverse_y),
        factor_x=f32(wave_factors(full_x)[:, None]),
        factor_y=f32(wave_factors(full_y)[None, :]),
        factor_z=f32(wave_factors(depth) + screening),
        masks=f32(masks.reshape(bricks_y * SLOTS, LANES)),
    )


def turn_of(slot):
    return (-PITCH * slot if slot < SIDE else 1 - PITCH * SIDE - SIDE * (slot - SIDE)) % LANES


def roll(values, shift, axis):
    shift = shift % values.shape[axis]
    return values if shift == 0 else pltpu.roll(values, shift, axis)


def dot(first, second, dims=((1,), (0,))):
    return lax.dot_general(
        first,
        second,
        (dims, ((), ())),
        precision=lax.Precision.HIGH,
        preferred_element_type=jnp.float32,
    )


def kernel(
    velocity_in, field_in, material_in, moments, nozzle_in, jet_in, inlet_in, rates_in, partners_in,
    basis_z_in, inverse_z_in, forward_x_in, backward_x_in, forward_y_in, backward_y_in,
    factor_x_in, factor_y_in, factor_z_in, masks_in,
    new_velocity, result,
    velocity, field, material, nozzle, jet, inlet, rates, partners,
    basis_z, inverse_z, forward_x, backward_x, forward_y, backward_y,
    factor_x, factor_y, factor_z, masks,
    ext, grown, face_x, face_y, cut_y, coef,
    edge_y, source, send_a, recv_a, send_b, recv_b, send_c, recv_c, send_d, recv_d, poten,
    load_sem, first_sem, later_sem, halo_send, halo_recv, ssem, rsem,
):
    wide = 16
    classes = rates.shape[1]
    rows = SIDE * SIDE
    me_x = lax.axis_index("gx")
    me_grp, me_gy = lax.axis_index("grp"), lax.axis_index("gy")
    groups = lax.axis_size("gy")
    me_y = me_grp * groups + me_gy
    levels = wide // CHAINS
    me_z = lax.rem(me_x, levels)
    me_sheet = me_x // levels * wide + me_y

    def along_x(index):
        return {"gx": index}

    def along_y(index):
        return {"grp": index // groups, "gy": lax.rem(index, groups)}

    def along_z(index):
        return {"gx": me_x - me_z + index}

    def in_sheet(index):
        line = lax.rem(index, wide)
        return {
            "gx": index // wide * levels + me_z,
            "grp": line // groups,
            "gy": lax.rem(line, groups),
        }

    first = [
        pltpu.make_async_copy(src, dst, first_sem.at[number])
        for number, (src, dst) in enumerate(
            [(velocity_in, velocity), (field_in, field), (material_in, material), (basis_z_in, basis_z)]
        )
    ]
    load = pltpu.make_async_copy(moments, ext.at[pl.ds(0, classes)], load_sem)
    later = [
        pltpu.make_async_copy(src, dst, later_sem.at[number])
        for number, (src, dst) in enumerate(
            [
                (nozzle_in, nozzle), (jet_in, jet), (inlet_in, inlet), (rates_in, rates),
                (partners_in, partners), (inverse_z_in, inverse_z), (forward_x_in, forward_x),
                (backward_x_in, backward_x), (forward_y_in, forward_y), (backward_y_in, backward_y),
                (factor_x_in, factor_x), (factor_y_in, factor_y), (factor_z_in, factor_z),
                (masks_in, masks),
            ]
        )
    ]
    for copy in first + [load] + later:
        copy.start()
    barrier = pltpu.get_barrier_semaphore()

    def greet(device):
        pl.semaphore_signal(barrier, inc=1, device_id=device, device_id_type=MESH)

    pl.loop(1, CHAINS * wide)(lambda k: greet(in_sheet(lax.rem(me_sheet + k, CHAINS * wide))))
    pl.loop(1, levels)(lambda k: greet(along_z(lax.rem(me_z + k, levels))))
    greet(along_x(lax.rem(me_x + 1, wide)))
    greet(along_x(lax.rem(me_x + wide - 1, wide)))

    lane = lax.broadcasted_iota(jnp.int32, (SIDE, LANES), 1)
    row = lax.broadcasted_iota(jnp.int32, (SIDE, LANES), 0)
    not_first, not_last = lane != 0, lane != LANES - 1

    def up_z(v):
        return jnp.where(not_last, roll(v, -1, 1), 0.0)

    def down_z(v):
        return jnp.where(not_first, roll(v, 1, 1), 0.0)

    def current_at(x):
        m = [ext[classes + a, SIDE * x : SIDE * x + SIDE] for a in range(3)]
        f = [field[a, x] for a in range(3)]
        return (
            m[1] * f[2] - m[2] * f[1],
            m[2] * f[0] - m[0] * f[2],
            m[0] * f[1] - m[1] * f[0],
        )

    for copy in first:
        copy.wait()

    for x in range(SIDE):
        liquid = material[x].astype(jnp.float32)
        for a in range(3):
            ext[classes + a, SIDE * x : SIDE * x + SIDE] = velocity[a, x] * liquid
    currents = [current_at(x) for x in range(SIDE)]
    for x in range(SIDE):
        c1, c2 = currents[x][1], currents[x][2]
        s = jnp.where(row < SIDE - 1, roll(c1, -1, 0), 0.0) - jnp.where(row > 0, roll(c1, 1, 0), 0.0)
        s = s + up_z(c2) - down_z(c2)
        if x + 1 < SIDE:
            s = s + currents[x + 1][0]
        if x > 0:
            s = s - currents[x - 1][0]
        source[PITCH * x + 1 : PITCH * x + 1 + SIDE] = 0.5 * s
        source[PITCH * x : PITCH * x + 1] = 0.5 * c1[0:1]
        source[PITCH * x + PITCH - 1 : PITCH * x + PITCH] = -0.5 * c1[SIDE - 1 : SIDE]
    edge = PITCH * SIDE
    source[edge : edge + SIDE] = 0.5 * currents[0][0]
    source[edge + SIDE : edge + 2 * SIDE] = -0.5 * currents[SIDE - 1][0]
    source[edge + 2 * SIDE :] = jnp.zeros((LANES - edge - 2 * SIDE, LANES), jnp.float32)
    send_a[...] = dot(basis_z[...], source[...], ((1,), (1,)))

    pl.semaphore_wait(barrier, CHAINS * wide + levels)

    def exchange(phase, send, recv, me, target, count, size):
        mine = pl.ds(pl.multiple_of(me * size, size), size)

        def start(step):
            other = lax.rem(me + step, count)
            pltpu.make_async_remote_copy(
                src_ref=send.at[pl.ds(pl.multiple_of(other * size, size), size)],
                dst_ref=recv.at[mine],
                send_sem=ssem.at[phase],
                recv_sem=rsem.at[phase],
                device_id=target(other),
                device_id_type=MESH,
            ).start()

        pl.loop(1, count)(start)
        recv[mine] = send[mine]

    def arrived(phase, recv, count, size):
        part = pl.ds(0, (count - 1) * size)
        pltpu.make_async_copy(recv.at[part], recv.at[part], rsem.at[phase]).wait()

    def sent(phase, send, count, size):
        part = pl.ds(0, (count - 1) * size)
        pltpu.make_async_copy(send.at[part], send.at[part], ssem.at[phase]).wait()

    sheet, column = (CHAINS * wide, SIDE), (levels, STRIDE)

    flat = ext.reshape((classes + 3) * rows, LANES)
    lower_x, upper_x = lax.rem(me_x + wide - 1, wide), lax.rem(me_x + 1, wide)
    lower_y, upper_y = lax.rem(me_y + wide - 1, wide), lax.rem(me_y + 1, wide)

    moment_faces = []

    def send_faces(copies, along, begin, count):
        part = pl.ds(begin, count)
        if along == "y":
            for side in range(2):
                cut_y[side, part] = flat[
                    pl.ds(begin * rows + side * (SIDE - 1), count * SIDE, stride=SIDE), :
                ].reshape(count, SIDE, LANES)
            jobs = (
                (cut_y.at[0, part], face_y.at[1, part], along_y(lower_y)),
                (cut_y.at[1, part], face_y.at[0, part], along_y(upper_y)),
            )
        else:
            jobs = (
                (ext.at[part, pl.ds(0, SIDE)], face_x.at[1, part], along_x(lower_x)),
                (ext.at[part, pl.ds(rows - SIDE, SIDE)], face_x.at[0, part], along_x(upper_x)),
            )
        for src, dst, device in jobs:
            number = len(moving_faces) + len(moment_faces)
            copy = pltpu.make_async_remote_copy(
                src_ref=src,
                dst_ref=dst,
                send_sem=halo_send.at[number],
                recv_sem=halo_recv.at[number],
                device_id=device,
                device_id_type=MESH,
            )
            copy.start()
            copies.append(copy)

    moving_faces = []
    exchange(0, send_a, recv_a, me_sheet, in_sheet, *sheet)
    send_faces(moving_faces, "y", classes, 3)
    send_faces(moving_faces, "x", classes, 3)
    load.wait()
    for copy in later:
        copy.wait()

    square = lax.broadcasted_iota(jnp.int32, (classes, LANES), 1)
    owner = lax.broadcasted_iota(jnp.int32, (classes, LANES), 0)
    label = lax.broadcasted_iota(jnp.int32, (classes, classes), 0)
    turned = jnp.zeros((classes, classes), jnp.float32)
    for r in range(rates.shape[0]):
        turned = turned + jnp.where(partners[r : r + 1] == label, rates[r : r + 1], 0.0)
    blank = jnp.zeros((classes, LANES - classes), jnp.float32)
    turned = jnp.concatenate([turned, blank], 1)
    full = jnp.concatenate([turned, jnp.zeros((LANES - classes, LANES), jnp.float32)], 0).T[:classes]
    low = jnp.where(square < owner, full + turned, jnp.where(square == owner, full, 0.0))
    full = full - jnp.where(owner == classes - 1, low, 0.0)
    low = jnp.where(owner > 0, roll(low, 1, 0), 0.0)
    both = jnp.concatenate([low, full], 0)
    high_part = both.astype(jnp.bfloat16).astype(jnp.float32)
    low_part = both - high_part
    place = lax.broadcasted_iota(jnp.int32, (2 * classes, LANES), 1)
    weights = jnp.where(place < classes, high_part, roll(low_part, classes, 1)).astype(jnp.bfloat16)
    flat_grown = grown.reshape(classes * rows, LANES)

    def grow(pair):
        parts = [
            flat[pl.ds(2 * pair + h, classes, stride=rows), :].astype(jnp.bfloat16) for h in range(2)
        ]
        narrow = jnp.concatenate(parts, 1)
        mixed = jnp.dot(
            weights, jnp.concatenate([narrow, narrow], 0), preferred_element_type=jnp.float32
        )
        for h in range(2):
            n = parts[h].astype(jnp.float32)
            piece = mixed[:, h * LANES : (h + 1) * LANES]
            flat_grown[pl.ds(2 * pair + h, classes, stride=rows), :] = (
                roll(n, 1, 0) * piece[:classes] - n * piece[classes:]
            )

    pl.loop(0, rows * 3 // 16, unroll=4)(grow)
    send_faces(moment_faces, "x", 0, 32)
    pl.loop(rows * 3 // 16, rows // 2, unroll=4)(grow)

    cell = lax.broadcasted_iota(jnp.int32, (rows, 1), 0)
    full_y = SIDE * wide
    base = ((me_x * SIDE + cell // SIDE) * full_y + me_y * SIDE + cell % SIDE) * LANES
    hit = [
        jnp.max(jnp.where(nozzle[...] == base + z, 1.0, 0.0), axis=1, keepdims=True) for z in range(2)
    ]
    deep = lax.broadcasted_iota(jnp.int32, (rows, LANES), 1)
    coef[8] = jnp.where(deep == 0, hit[0], jnp.where(deep == 1, hit[1], 0.0))

    arrived(0, recv_a, *sheet)
    for chain in range(CHAINS):
        strips = [jnp.zeros((levels, LANES), jnp.float32) for _ in range(PITCH)]
        for by in range(wide):
            place = (chain * wide + by) * SIDE
            line = roll(recv_a[place : place + SIDE], SIDE * by - 1, 1)
            for slot in range(PITCH):
                strips[slot] = strips[slot] + line * masks[by * SLOTS + slot : by * SLOTS + slot + 1]
        for slot in range(PITCH):
            send_b[pl.ds(chain * PITCH + slot, levels, stride=STRIDE), :] = roll(
                strips[slot], turn_of(slot), 1
            )
    for slot in range(CHAINS * PITCH, STRIDE):
        send_b[pl.ds(slot, levels, stride=STRIDE), :] = jnp.zeros((levels, LANES), jnp.float32)
    exchange(1, send_b, recv_b, me_z, along_z, *column)
    send_faces(moment_faces, "y", 0, 32)

    for copy in moving_faces:
        copy.wait_recv()
    has_x = [(me_x > 0).astype(jnp.float32), (me_x < wide - 1).astype(jnp.float32)]
    has_y = [(me_y > 0).astype(jnp.float32), (me_y < wide - 1).astype(jnp.float32)]

    def moving_at(a, x):
        if x < 0:
            return face_x[0, classes + a] * has_x[0]
        if x >= SIDE:
            return face_x[1, classes + a] * has_x[1]
        return ext[classes + a, SIDE * x : SIDE * x + SIDE]

    def around_y(a, x):
        here = moving_at(a, x)
        below = jnp.where(row == 0, face_y[0, classes + a, x : x + 1] * has_y[0], roll(here, 1, 0))
        above = jnp.where(
            row == SIDE - 1, face_y[1, classes + a, x : x + 1] * has_y[1], roll(here, -1, 0)
        )
        return below, above

    for x in range(SIDE):
        part = slice(SIDE * x, SIDE * x + SIDE)
        stop = coef[8, part]
        scale = step_size * material[x].astype(jnp.float32) * (1.0 - stop)
        total = jnp.zeros((SIDE, LANES), jnp.float32)
        for a in range(3):
            here = moving_at(a, x)
            if a == 0:
                below, above = moving_at(0, x - 1), moving_at(0, x + 1)
            elif a == 1:
                below, above = around_y(1, x)
            else:
                below, above = down_z(here), up_z(here)
            up, down = 0.5 * (here + above), 0.5 * (below + here)
            total = total + (jnp.maximum(up, 0.0) - jnp.minimum(down, 0.0))
            plus, minus = -scale * jnp.minimum(up, 0.0), scale * jnp.maximum(down, 0.0)
            if a == 0:
                if x == 0:
                    minus = minus * has_x[0]
                if x == SIDE - 1:
                    plus = plus * has_x[1]
            elif a == 1:
                edge_y[0, x : x + 1] = minus[0:1] * has_y[0]
                edge_y[1, x : x + 1] = plus[SIDE - 1 : SIDE] * has_y[1]
                minus = jnp.where(row == 0, 0.0, minus)
                plus = jnp.where(row == SIDE - 1, 0.0, plus)
            else:
                minus = jnp.where(not_first, minus, 0.0)
                plus = jnp.where(not_last, plus, 0.0)
            coef[2 * a + 1, part] = minus
            coef[2 * a + 2, part] = plus
        coef[0, part] = 1.0 - stop - scale * total
        coef[7, part] = scale

    flat_result = result.reshape(classes * rows, LANES)

    def advance(k):
        fill = inlet[k]
        for x in range(SIDE):
            part = slice(SIDE * x, SIDE * x + SIDE)
            here = ext[k, part]
            value = (
                (coef[0, part] * here + coef[7, part] * grown[k, part])
                + (coef[3, part] * roll(here, 1, 0) + coef[4, part] * roll(here, -1, 0))
                + (coef[5, part] * roll(here, 1, 1) + coef[6, part] * roll(here, -1, 1))
                + coef[8, part] * fill
            )
            if x > 0:
                value = value + coef[1, part] * ext[k, SIDE * x - SIDE : SIDE * x]
            if x < SIDE - 1:
                value = value + coef[2, part] * ext[k, SIDE * x + SIDE : SIDE * x + 2 * SIDE]
            result[k, part] = value

    def finish_x(k):
        for side, start in ((0, 0), (1, rows - SIDE)):
            part = slice(start, start + SIDE)
            result[k, part] = result[k, part] + coef[1 + side, part] * face_x[side, k]

    def finish_y(k):
        for side in range(2):
            part = pl.ds(k * rows + side * (SIDE - 1), SIDE, stride=SIDE)
            flat_result[part, :] = flat_result[part, :] + edge_y[side] * face_y[side, k]

    pl.loop(0, classes, unroll=2)(advance)

    wave = factor_z[me_sheet * levels + me_z]
    inverse = -1.0 / ((factor_x[...] + wave) + factor_y[...])
    arrived(1, recv_b, *column)
    plane = dot(dot(forward_x[...], recv_b[...]), forward_y[...]) * inverse
    send_c[...] = dot(backward_x[...], dot(plane, backward_y[...]))
    exchange(2, send_c, recv_c, me_z, along_z, *column)
    send_faces(moment_faces, "y", 32, 32)
    for x in range(SIDE):
        part = slice(SIDE * x, SIDE * x + SIDE)
        c = current_at(x)
        f = [field[a, x] for a in range(3)]
        lorentz = (c[1] * f[2] - c[2] * f[1], c[2] * f[0] - c[0] * f[2], c[0] * f[1] - c[1] * f[0])
        liquid = material[x].astype(jnp.float32)
        stop = coef[8, part] > 0.5
        for a in range(3):
            here = moving_at(a, x)
            below, above = around_y(a, x)
            spread = (
                (moving_at(a, x - 1) + moving_at(a, x + 1))
                + (below + above)
                + (down_z(here) + up_z(here))
                - 6.0 * here
            )
            value = liquid * (here + step_size * (lorentz[a] + viscosity * spread))
            new_velocity[a, x] = jnp.where(stop, jet[a], value)

    arrived(2, recv_c, *column)
    for chain in range(CHAINS):
        strips = [
            roll(recv_c[pl.ds(chain * PITCH + slot, levels, stride=STRIDE), :], -turn_of(slot), 1)
            for slot in range(PITCH)
        ]
        for by in range(wide):
            total = jnp.zeros((levels, LANES), jnp.float32)
            for slot in range(PITCH):
                total = total + strips[slot] * masks[by * SLOTS + slot : by * SLOTS + slot + 1]
            place = (chain * wide + by) * SIDE
            send_d[place : place + SIDE] = roll(total, 1 - SIDE * by, 1)
    exchange(3, send_d, recv_d, me_sheet, in_sheet, *sheet)
    send_faces(moment_faces, "x", 32, 32)

    for copy in moment_faces[:4]:
        copy.wait_recv()
    pl.loop(0, classes // 2, unroll=4)(finish_x)
    pl.loop(0, classes // 2, unroll=4)(finish_y)
    for copy in moment_faces[4:6]:
        copy.wait_recv()
    pl.loop(classes // 2, classes, unroll=4)(finish_y)

    arrived(3, recv_d, *sheet)
    poten[...] = dot(recv_d[...], inverse_z[...], ((0,), (0,)))
    for x in range(SIDE):
        part = slice(SIDE * x, SIDE * x + SIDE)

        def pot(x):
            if x < 0:
                return poten[edge : edge + SIDE]
            if x >= SIDE:
                return poten[edge + SIDE : edge + 2 * SIDE]
            return poten[PITCH * x + 1 : PITCH * x + 1 + SIDE]

        low_y = poten[PITCH * x : PITCH * x + SIDE]
        high_y = poten[PITCH * x + 2 : PITCH * x + 2 + SIDE]
        middle = pot(x)
        gradient = (
            0.5 * (pot(x + 1) - pot(x - 1)),
            0.5 * (high_y - low_y),
            0.5 * (up_z(middle) - down_z(middle)),
        )
        f = [field[a, x] for a in range(3)]
        pull = (
            gradient[1] * f[2] - gradient[2] * f[1],
            gradient[2] * f[0] - gradient[0] * f[2],
            gradient[0] * f[1] - gradient[1] * f[0],
        )
        for a in range(3):
            new_velocity[a, x] = new_velocity[a, x] - coef[7, part] * pull[a]

    for copy in moment_faces[6:]:
        copy.wait_recv()
    pl.loop(classes // 2, classes, unroll=4)(finish_x)

    for phase, buffer, shape in (
        (0, send_a, sheet), (1, send_b, column), (2, send_c, column), (3, send_d, sheet),
    ):
        sent(phase, buffer, *shape)
    for copy in moving_faces + moment_faces:
        copy.wait_send()


def local(velocity, moments, field, material, nozzle, jet, inlet, rates, partners):
    width_x = lax.axis_size("gx")
    width_y = lax.axis_size("grp") * lax.axis_size("gy")
    cells_x, cells_y, depth = material.shape
    classes = moments.shape[0]
    rows = cells_x * cells_y
    table = tables(cells_x * width_x, cells_y * width_y, depth)
    f32 = jnp.float32
    operands = (
        velocity, field, material, moments.reshape(classes, rows, depth),
        nozzle.reshape(1, -1), jet, inlet, rates.T, partners.T,
        table["basis_z"], table["inverse_z"], table["forward_x"], table["backward_x"],
        table["forward_y"], table["backward_y"], table["factor_x"], table["factor_y"],
        table["factor_z"], table["masks"],
    )
    scalars = (5, 6, 17)
    here = [
        (pltpu.SMEM if number in scalars else pltpu.VMEM)(array.shape, array.dtype)
        for number, array in enumerate(operands)
        if number != 3
    ]
    vmem = pl.BlockSpec(memory_space=pltpu.VMEM)
    far = pl.BlockSpec(memory_space=pltpu.HBM)
    square = pltpu.VMEM((2 * LANES, LANES), f32)
    narrow = pltpu.VMEM((width_x // CHAINS * STRIDE, LANES), f32)
    faces = pltpu.VMEM((2, classes + 3, SIDE, LANES), f32)
    new_velocity, new_moments = pl.pallas_call(
        kernel,
        out_shape=(
            pltpu.VMEM(velocity.shape, f32),
            pltpu.VMEM((classes, rows, depth), f32),
        ),
        in_specs=[far] * len(operands),
        out_specs=(vmem, vmem),
        scratch_shapes=here + [
            pltpu.VMEM((classes + 3, rows, LANES), f32),
            pltpu.VMEM((classes, rows, LANES), f32),
            faces, faces, faces,
            pltpu.VMEM((9, rows, LANES), f32),
            pltpu.VMEM((2, SIDE, LANES), f32),
            pltpu.VMEM((LANES, LANES), f32),
            square, square, narrow, narrow, narrow, narrow, square, square,
            pltpu.VMEM((LANES, LANES), f32),
            pltpu.SemaphoreType.DMA,
            pltpu.SemaphoreType.DMA((4,)),
            pltpu.SemaphoreType.DMA((14,)),
            pltpu.SemaphoreType.DMA((16,)),
            pltpu.SemaphoreType.DMA((16,)),
            pltpu.SemaphoreType.DMA((4,)),
            pltpu.SemaphoreType.DMA((4,)),
        ],
        compiler_params=pltpu.CompilerParams(
            collective_id=0, has_side_effects=True, vmem_limit_bytes=60 * 1024 * 1024
        ),
    )(*operands)
    return (new_velocity, new_moments.reshape(moments.shape))


def solution(mesh):
    bricks = P(None, "gx", ("grp", "gy"), None)
    return jax.shard_map(
        local,
        mesh=mesh,
        in_specs=(bricks, bricks, bricks, P("gx", ("grp", "gy"), None), P(), P(), P(), P(), P()),
        out_specs=(bricks, bricks),
        check_vma=False,
    )
```
